512 devices in a mesh: dp: 16 (over z), seq: 32 (over x, y, core).
Axes of the slice: x: 4, y: 4, z: 16, core: 2. Of those that a mesh axis runs over, the one named last changes fastest.
Arguments:
- inputs: bfloat16 [16, 32, 256, 256], P('dp', 'seq'), may hold values from -6 to 6
- cotangent: bfloat16 [16, 32, 256, 256], P('dp', 'seq'), may hold values from -6 to 6
- lengths: int32 [16, 8], P('dp'), may hold values from 1 to 2048, 8192 in all within a row
- placed: int32 [16, 32], P('dp'), may hold values from 0 to 31, each once within a row
- conv_weight: float32 [51, 256], replicated, may hold values from -0.875 to 0.875
- norm_gain: float32 [256], replicated, may hold values from 0.5 to 1.5
- up_weight: bfloat16 [256, 1024], replicated, may hold values from -0.375 to 0.375
- down_weight: bfloat16 [1024, 256], replicated, may hold values from -0.1875 to 0.1875
Outputs:
- outputs: bfloat16 [16, 32, 256, 256], P('dp', 'seq')
- grad_inputs: bfloat16 [16, 32, 256, 256], P('dp', 'seq')
- grad_kernel: bfloat16 [51, 256], replicated
- grad_gain: bfloat16 [256], replicated
- grad_up: bfloat16 [256, 1024], replicated
- grad_down: bfloat16 [1024, 256], replicated
The draws below stay inside these ranges and needn't reach their ends.
Inputs may be any that keep to these rules, and one draw needn't show every extreme that they name: `lengths`: each trace has at least one step and together they fill the group's 256 * 32 steps. `placed`: each row is a permutation of the span numbers.
All inputs are finite; a program needn't handle non-finite values.
Results may differ from the reference program's by a relative error of at most 0.0061.
Values may be sent and summed in bfloat16 or wider, within the bound.
A program may use at most 64 MiB of HBM per device.

```python
import math
import jax
import jax.numpy as jnp
import numpy as np
from jax import lax

C = 256
HID = 1024
K = 51
ROWS = 256
TRACES = 8
SPANS = 32
GROUPS = 16


def shard_levels(own_key, shape, cuts, smallest, largest):
    factor_of = 1.0
    for position, blocks in cuts:
        steps = jax.random.uniform(jax.random.fold_in(jax.random.fold_in(own_key, 6), position), (blocks,), jnp.float32, smallest / len(cuts), largest / len(cuts))
        factor_of = factor_of * jnp.repeat(jnp.exp(steps), shape[position] // blocks).reshape((-1,) + (1,) * (len(shape) - 1 - position))
    return factor_of


def length_profile(count, total, reach, skew):
    loads = [(1 << 20) // math.isqrt(rank ** skew) + 1 for rank in range(2, count + 1)]
    surplus, given = total - reach - (count - 1), [1] * (count - 1)
    while surplus > 0:
        candidates = [i for i in range(count - 1) if given[i] < reach]
        pool, budget = sum([loads[i] for i in candidates]), surplus
        for i in candidates:
            extra = min(reach - given[i], max(1, budget * loads[i] // pool), surplus)
            given[i] = given[i] + extra
            surplus = surplus - extra
    return np.array([reach] + given)


def uneven_parts(own_key, number_of, total, reach, lean):
    if number_of == 2:
        one = jax.random.randint(own_key, (), max(1, total - reach), min(reach, total - 1) + 1)
        return jnp.stack([one, total - one])
    sizes = jnp.asarray(length_profile(number_of, total, reach, lean), jnp.int32)
    twos = (number_of - 1) // 2
    giver, taker = sizes[1:1 + 2 * twos:2], sizes[2:2 + 2 * twos:2]
    room = jnp.minimum(giver - 1, reach - taker)
    shifted = jax.random.randint(jax.random.fold_in(own_key, 1), (twos,), 0, 1 << 20) % (room + 1)
    sizes = sizes.at[1:1 + 2 * twos:2].set(giver - shifted).at[2:2 + 2 * twos:2].set(taker + shifted)
    return sizes[jax.random.permutation(jax.random.fold_in(own_key, 2), number_of)]


def scatter_about(stream_key, extent, deviation, limit, cuts=(), kind=jnp.bfloat16):
    drawn = jax.random.normal(stream_key, extent, jnp.float32) * deviation
    if len(cuts) > 0:
        drawn = shard_levels(stream_key, extent, cuts, -0.22, 0.18) * drawn
    return jnp.clip(drawn, min=-limit, max=limit).astype(kind)


def setup_inputs(seed: int = 0) -> dict:
    keys = jax.random.split(jax.random.key(seed), 9)
    return {
        "inputs": scatter_about(keys[0], (GROUPS, SPANS, ROWS, C), 1.0, 6.0, ((0, 16), (1, 32))),
        "cotangent": scatter_about(keys[1], (GROUPS, SPANS, ROWS, C), 1.0, 6.0, ((0, 16), (1, 32))),
        "lengths": jax.vmap(lambda own: uneven_parts(own, TRACES, ROWS * SPANS, ROWS * SPANS // 4, 2))(jax.random.split(keys[2], GROUPS)).reshape((GROUPS, TRACES)).astype(jnp.int32),
        "placed": jax.vmap(lambda own: jax.random.permutation(own, SPANS))(jax.random.split(keys[3], GROUPS)).reshape((GROUPS, SPANS)).astype(jnp.int32),
        "conv_weight": scatter_about(keys[4], (K, C), K ** -0.5, 0.875, (), jnp.float32),
        "norm_gain": jnp.clip(1.0 + 0.1 * jax.random.normal(keys[5], (C,), jnp.float32), 0.5, 1.5),
        "up_weight": scatter_about(keys[6], (C, HID), C ** -0.5, 0.375),
        "down_weight": scatter_about(keys[7], (HID, C), HID ** -0.5, 0.1875),
    }


epsilon = 1e-05

def depth_rows(positions, lengths):
    trace_ends = jnp.cumsum(lengths).astype(jnp.int32)
    trace_start = lax.optimization_barrier(jnp.sum(jnp.where(trace_ends[None, :] <= positions[:, None], lengths[None, :], 0), axis=1)).astype(jnp.int32)
    return positions - trace_start

def contract_rows(left, right):
    return lax.dot_general(left, right, (((0,), (0,)), ((), ())), preferred_element_type=jnp.float32)

def contract_cols(left, right):
    return lax.dot_general(left, right, (((1,), (1,)), ((), ())), preferred_element_type=jnp.float32)

def reference(inputs, cotangent, lengths, placed, conv_weight, norm_gain, up_weight, down_weight):
    reach_rows = K - 1
    total = ROWS * SPANS

    def one_group(group_args):
        x_slots, dy_slots, group_lengths, order_row = group_args
        slot_of = jnp.zeros((SPANS,), jnp.int32).at[order_row].set(jnp.arange(SPANS, dtype=jnp.int32))
        series = x_slots[slot_of].reshape(total, C)
        upstream = dy_slots[slot_of].reshape(total, C)
        positions = jnp.arange(total, dtype=jnp.int32)
        depth = depth_rows(positions, group_lengths)
        extended = jnp.concatenate([jnp.zeros((reach_rows, C), jnp.bfloat16), series], axis=0)
        conv_out = jnp.zeros((total, C), jnp.float32)
        for offset in range(K):
            window = extended[reach_rows - offset:reach_rows - offset + total].astype(jnp.float32)
            conv_out = conv_out + jnp.where((offset <= depth)[:, None], conv_weight[offset] * window, 0.0)
        centre = lax.optimization_barrier(jnp.mean(conv_out, axis=-1, keepdims=True))
        centered = conv_out - centre
        variance = lax.optimization_barrier(jnp.mean(centered * centered, axis=-1, keepdims=True))
        inv_std = lax.rsqrt(variance + epsilon)
        normed = centered * inv_std
        scaled = (normed * norm_gain).astype(jnp.bfloat16)
        hidden = jnp.dot(scaled, up_weight, preferred_element_type=jnp.float32)
        activated = jax.nn.gelu(hidden).astype(jnp.bfloat16)
        result = (series.astype(jnp.float32) + jnp.dot(activated, down_weight, preferred_element_type=jnp.float32)).astype(jnp.bfloat16)
        grad_down = contract_rows(activated, upstream)
        grad_act = contract_cols(upstream, down_weight)
        pullback = jax.vjp(jax.nn.gelu, hidden)[1]
        grad_hidden = pullback(grad_act)[0].astype(jnp.bfloat16)
        grad_up = contract_rows(scaled, grad_hidden)
        grad_normed = contract_cols(grad_hidden, up_weight)
        grad_gain = lax.optimization_barrier(jnp.sum(grad_normed * normed, axis=0))
        weighted = grad_normed * norm_gain
        grad_conv_out = inv_std * (weighted - lax.optimization_barrier(jnp.mean(weighted, axis=-1, keepdims=True)) - normed * lax.optimization_barrier(jnp.mean(weighted * normed, axis=-1, keepdims=True)))
        padded_grad = jnp.concatenate([grad_conv_out, jnp.zeros((reach_rows, C), jnp.float32)], axis=0)
        padded_depth = jnp.concatenate([depth, jnp.zeros((reach_rows,), jnp.int32)], axis=0)
        grad_through = jnp.zeros((total, C), jnp.float32)
        kernel_rows = []
        for offset in range(K):
            ahead = padded_grad[offset:offset + total]
            grad_through = grad_through + jnp.where((offset <= padded_depth[offset:offset + total])[:, None], conv_weight[offset] * ahead, 0.0)
            window = extended[reach_rows - offset:reach_rows - offset + total].astype(jnp.float32)
            kernel_rows.append(lax.optimization_barrier(jnp.sum(jnp.where((offset <= depth)[:, None], grad_conv_out * window, 0.0), axis=0)))
        grad_kernel = jnp.stack(kernel_rows, axis=0)
        grad_series = (upstream.astype(jnp.float32) + grad_through).astype(jnp.bfloat16)
        out_slots = result.reshape(SPANS, ROWS, C)[order_row]
        grad_slots = grad_series.reshape(SPANS, ROWS, C)[order_row]
        return (out_slots, grad_slots, grad_kernel, grad_gain, grad_up, grad_down)
    out_all, grad_all, kernel_all, gain_all, up_all, down_all = lax.map(one_group, (inputs, cotangent, lengths, placed))
    factor = 1.0 / math.sqrt(GROUPS * SPANS * ROWS)
    return (out_all, grad_all, (lax.optimization_barrier(jnp.sum(kernel_all, axis=0)) * factor).astype(jnp.bfloat16), (lax.optimization_barrier(jnp.sum(gain_all, axis=0)) * factor).astype(jnp.bfloat16), (lax.optimization_barrier(jnp.sum(up_all, axis=0)) * factor).astype(jnp.bfloat16), (lax.optimization_barrier(jnp.sum(down_all, axis=0)) * factor).astype(jnp.bfloat16))
```

```python
import math

import jax
import jax.numpy as jnp
from jax import lax
from jax.experimental import pallas as pl
from jax.experimental.pallas import tpu as pltpu
from jax.sharding import PartitionSpec as P

MESH = pl.DeviceIdType.MESH
F32 = jnp.float32
BF16 = jnp.bfloat16

EPS = 1e-05
C = 256
HID = 1024
K = 51
ROWS = 256
TRACES = 8
HALO = 64
BLK = 64
NZ, NSEQ, NQ = 16, 32, 16
CH = 4
FACTOR = 1.0 / math.sqrt(NZ * NSEQ * ROWS)
GELU_C = math.sqrt(2.0 / math.pi)
GELU_A = 0.044715


def dot(a, b, ca, cb):
    return lax.dot_general(a, b, (((ca,), (cb,)), ((), ())), preferred_element_type=F32)


def remote(src, dst, send, recv, dev):
    return pltpu.make_async_remote_copy(
        src_ref=src, dst_ref=dst, send_sem=send, recv_sem=recv, device_id=dev, device_id_type=MESH
    )


def loop(lo, hi, body):
    def step(i, carry):
        body(i)
        return carry

    lax.fori_loop(lo, hi, step, 0)


def kernel(
    lengths, placed, x_ref, dy_ref, w_ref, gain_ref, up_hbm, down_hbm,
    out_ref, gin_ref, gk_ref, gg_ref, gu_hbm, gd_hbm,
    up_v, down_v, gath0, gath1, send_b, recv0, recv1, head, ext, gext, dep, rem_, normed_s, istd_s, scaled_s,
    gn_s, oacc_s, own, outbound, sib, tsum, r1, zs, r2, a1, fin, kp, kb, rk, rz, kf,
    ld_sem, a_s, a_r, b_s, b_r, c_s, c_r, p_s, p_r, z_s, z_r, y_s, y_r, q_s, q_r, f_s, f_r,
    k_s, k_r, kz_s, kz_r, kf_s, kf_r, st_sem,
):
    z = lax.axis_index("dp")
    s = lax.axis_index("seq")
    core = lax.rem(s, 2)
    q = lax.div(s, 2)
    yy = lax.rem(q, 4)
    xx = lax.div(q, 4)
    g = xx * 2 + core
    sibling = (z, q * 2 + 1 - core)
    gath, recv = (gath0, gath1), (recv0, recv1)

    bar = pltpu.get_barrier_semaphore()
    loop(1, NSEQ, lambda i: pl.semaphore_signal(
        bar, inc=1, device_id=(z, lax.rem(s + i, NSEQ)), device_id_type=MESH))
    loop(1, NZ, lambda i: pl.semaphore_signal(
        bar, inc=1, device_id=(lax.rem(z + i, NZ), s), device_id_type=MESH))
    loads = [
        pltpu.make_async_copy(up_hbm, up_v, ld_sem.at[0]),
        pltpu.make_async_copy(down_hbm, down_v, ld_sem.at[1]),
    ]
    for copy in loads:
        copy.start()

    def target(i):
        gt = lax.rem(g + i, 8)
        return (lax.div(gt, 2) * 4 + yy) * 2 + lax.rem(gt, 2)

    targets = [target(i) for i in range(8)]
    at = [placed[0, t] for t in targets]

    def look(k, found):
        p = placed[0, k]
        return tuple(
            jnp.where(p == at[i % 8] + (-1 if i < 8 else 1), k, f) for i, f in enumerate(found)
        )

    found = lax.fori_loop(0, NSEQ, look, (jnp.int32(0),) * 16)
    before, after = found[:8], found[8:]

    def y_of(slot):
        return lax.rem(lax.div(slot, 2), 4)

    def g_of(slot):
        return lax.div(slot, 8) * 2 + lax.rem(slot, 2)

    pl.semaphore_wait(bar, NSEQ - 1 + NZ - 1)

    def phase_a(d, src):
        def copy(i):
            peer = (xx * 4 + lax.rem(yy + i, 4)) * 2 + core
            return remote(src, gath[d].at[yy], a_s.at[d, i], a_r.at[d, i], (z, peer))

        for i in range(1, 4):
            copy(i).start()
        gath[d][yy] = src[...]

    def phase_a_wait(d):
        for i in range(1, 4):
            slot = gath[d].at[lax.rem(yy + 4 - i, 4)]
            remote(slot, slot, a_s.at[d, i], a_r.at[d, i], sibling).wait_recv()

    def phase_b(d, source):
        for i in range(1, 8):
            send_b[d, i] = gath[d][y_of(source[i])]
            remote(send_b.at[d, i], recv[d].at[g], b_s.at[d, i], b_r.at[d, i], (z, targets[i])).start()
        recv[d][g] = gath[d][y_of(source[0])]

    def phase_b_wait(d, source):
        for i in range(1, 8):
            slot = recv[d].at[lax.rem(g + 8 - i, 8)]
            remote(slot, slot, b_s.at[d, i], b_r.at[d, i], sibling).wait_recv()
        return recv[d][g_of(source[0])].astype(F32)

    tail = x_ref.at[pl.ds(ROWS - HALO, HALO), :]
    phase_a(0, tail)

    pos = at[0] * ROWS + lax.broadcasted_iota(jnp.int32, (ROWS, 128), 0)
    ends, end = [], jnp.int32(0)
    for i in range(TRACES):
        end = end + lengths[0, i]
        ends.append(end)
    start = jnp.zeros((ROWS, 128), jnp.int32)
    for e in ends:
        start = jnp.where(e <= pos, e, start)
    dep[...] = pos - start
    stop = jnp.zeros((ROWS, 128), jnp.int32)
    for e in reversed(ends):
        stop = jnp.where(e > pos, e, stop)
    rem_[...] = stop - 1 - pos

    for hf in range(2):
        ext[hf, HALO:, :] = x_ref[:, hf * 128:(hf + 1) * 128].astype(F32)

    phase_a_wait(0)
    phase_b(0, before)

    def depthwise(src, base, sign, mask_ref, r0):
        m = mask_ref[r0:r0 + BLK, :]
        acc = [jnp.zeros((BLK, 128), F32) for _ in range(2)]
        for j in range(K):
            lo = base + r0 + sign * j
            inside = m >= j
            for hf in range(2):
                win = src[hf, lo:lo + BLK, :] * w_ref[j:j + 1, hf * 128:(hf + 1) * 128]
                acc[hf] = acc[hf] + jnp.where(inside, win, 0.0)
        return acc

    def forward_block(r0):
        a0, a1_ = depthwise(ext, HALO, -1, dep, r0)
        mean = (jnp.sum(a0, axis=1, keepdims=True) + jnp.sum(a1_, axis=1, keepdims=True)) * (1.0 / C)
        a0, a1_ = a0 - mean, a1_ - mean
        var = (jnp.sum(a0 * a0, axis=1, keepdims=True) + jnp.sum(a1_ * a1_, axis=1, keepdims=True)) * (1.0 / C)
        inv = lax.rsqrt(var + EPS)
        istd_s[r0:r0 + BLK, :] = jnp.broadcast_to(inv, (BLK, 128))
        for hf, a in enumerate((a0, a1_)):
            cols = slice(hf * 128, (hf + 1) * 128)
            n = a * inv
            normed_s[r0:r0 + BLK, cols] = n
            scaled_s[r0:r0 + BLK, cols] = (n * gain_ref[0:1, cols]).astype(BF16)

    for r0 in range(BLK, ROWS, BLK):
        forward_block(r0)
    halo = phase_b_wait(0, before)
    for hf in range(2):
        ext[hf, :HALO, :] = halo[:, hf * 128:(hf + 1) * 128]
    forward_block(0)

    for copy in loads:
        copy.wait()

    def chip(k):
        qp = lax.rem(xx + lax.div(k, 4), 4) * 4 + lax.rem(yy + lax.rem(k, 4), 4)
        return qp

    def chip_back(k):
        return lax.rem(xx + 4 - lax.div(k, 4), 4) * 4 + lax.rem(yy + 4 - lax.rem(k, 4), 4)

    def rows16(i):
        return pl.ds(pl.multiple_of(i * 16, 16), 16)

    def mlp_chunk(h):
        cols = slice(h * 256, (h + 1) * 256)
        up_c = up_v[:, cols]
        down_c = down_v[cols, :]
        hid = dot(scaled_s[...], up_c, 1, 0)
        gact = dot(dy_ref[...], down_c, 1, 1)
        h2 = hid * hid
        th = jnp.tanh(hid * (GELU_C + (GELU_C * GELU_A) * h2))
        h1 = 0.5 + 0.5 * th
        act = hid * h1
        slope = h1 + act * (1.0 - th) * (GELU_C + (3.0 * GELU_C * GELU_A) * h2)
        act = act.astype(BF16)
        gh = (gact * slope).astype(BF16)
        o = dot(act, down_c, 1, 0)
        n = dot(gh, up_c, 1, 1)
        if h == 0:
            oacc_s[...] = o
            gn_s[...] = n
        else:
            oacc_s[...] += o
            gn_s[...] += n
        gdown = dot(act, dy_ref[...], 0, 0)
        gup = dot(scaled_s[...], gh, 0, 0)
        first = core == 0
        own[h] = jnp.where(first, gdown, gup)
        outbound[h] = jnp.where(first, gup, gdown).astype(BF16)
        remote(outbound.at[h], sib.at[h], c_s.at[h], c_r.at[h], sibling).start()

    def pair_stage(h):
        remote(sib.at[h], sib.at[h], c_s.at[h], c_r.at[h], sibling).wait_recv()
        tsum[h] = (own[h] + sib[h].astype(F32)).astype(BF16)

        def send(k):
            qp = chip(k)
            remote(tsum.at[h, rows16(qp), :], r1.at[h, k], p_s.at[h, k], p_r.at[h, k],
                   (z, qp * 2 + core)).start()

        loop(1, NQ, send)

    for h in range(CH):
        mlp_chunk(h)
        if h:
            pair_stage(h - 1)
    out_ref[...] = (x_ref[...].astype(F32) + oacc_s[...]).astype(BF16)
    pair_stage(CH - 1)

    ggain = jnp.zeros((1, C), F32)
    for r0 in range(0, ROWS, BLK):
        gn = gn_s[r0:r0 + BLK, :]
        nm = normed_s[r0:r0 + BLK, :]
        ggain = ggain + jnp.sum(gn * nm, axis=0, keepdims=True)
        qv = gn * gain_ref[...]
        m1 = jnp.sum(qv, axis=1, keepdims=True) * (1.0 / C)
        m2 = jnp.sum(qv * nm, axis=1, keepdims=True) * (1.0 / C)
        t = qv - m1 - nm * m2
        for hf in range(2):
            gext[hf, r0:r0 + BLK, :] = t[:, hf * 128:(hf + 1) * 128] * istd_s[r0:r0 + BLK, :]
    for hf in range(2):
        head[:, hf * 128:(hf + 1) * 128] = gext[hf, :HALO, :].astype(BF16)
    phase_a(1, head)

    for r0 in range(0, ROWS, BLK):
        m = dep[r0:r0 + BLK, :]
        gc = [gext[hf, r0:r0 + BLK, :] for hf in range(2)]
        for j in range(K):
            lo = HALO + r0 - j
            inside = m >= j
            for hf in range(2):
                v = jnp.where(inside, gc[hf] * ext[hf, lo:lo + BLK, :], 0.0)
                part = jnp.sum(v.reshape(BLK // 8, 8, 128), axis=0)
                if r0 == 0:
                    kp[hf, j] = part
                else:
                    kp[hf, j] += part
    for hf in range(2):
        taps = jnp.sum(kp[hf], axis=1)
        taps = jnp.concatenate(
            [taps, ggain[:, hf * 128:(hf + 1) * 128], jnp.zeros((64 - K - 1, 128), F32)], axis=0)
        for r in range(8):
            kb[2 * r + hf] = taps[r * 8:r * 8 + 8, :]

    def send_k(i):
        p = lax.rem(q + i, NQ)
        return remote(kb.at[p], rk.at[s], k_s.at[i], k_r.at[s], (z, p * 2))

    loop(1, NQ, lambda i: send_k(i).start())

    @pl.when(core == 1)
    def _():
        send_k(0).start()

    for h in range(CH):
        def got(k, h=h):
            remote(r1.at[h, k], r1.at[h, k], p_s.at[h, k], p_r.at[h, k], sibling).wait_recv()

        loop(1, NQ, got)
        acc = tsum[h, rows16(q), :].astype(F32)
        for k in range(1, NQ):
            acc = acc + r1[h, k].astype(F32)
        for rh in range(2):
            for hf in range(2):
                zs[h * 4 + rh * 2 + hf] = acc[rh * 8:rh * 8 + 8, hf * 128:(hf + 1) * 128]

    def send_z(i):
        zp = lax.rem(z + i, NZ)
        return remote(zs.at[zp], r2.at[i], z_s.at[i], z_r.at[i], (zp, s))

    loop(1, NZ, lambda i: send_z(i).start())

    phase_a_wait(1)
    phase_b(1, after)

    def back_block(r0):
        acc = depthwise(gext, 0, 1, rem_, r0)
        for hf in range(2):
            cols = slice(hf * 128, (hf + 1) * 128)
            gin_ref[r0:r0 + BLK, cols] = (dy_ref[r0:r0 + BLK, cols].astype(F32) + acc[hf]).astype(BF16)

    back_block(0)

    loop(1, NZ, lambda i: send_z(i).wait_recv())
    total = zs[z]
    for i in range(1, NZ):
        total = total + r2[i]
    a1[z] = total * FACTOR

    def send_y(i):
        return remote(a1.at[z], a1.at[z], y_s.at[i], y_r.at[i], (lax.rem(z + i, NZ), s))

    loop(1, NZ, lambda i: send_y(i).start())

    @pl.when(core == 0)
    def _():
        def got(i):
            sp = lax.rem(s + i, NSEQ)
            remote(rk.at[sp], rk.at[sp], k_s.at[0], k_r.at[sp], sibling).wait_recv()

        loop(1, NSEQ, got)
        rk[s] = kb[q]
        acc = rk[0]
        for i in range(1, NSEQ):
            acc = acc + rk[i]
        rz[z] = acc
        loop(1, NZ, lambda i: remote(
            rz.at[z], rz.at[z], kz_s.at[i], kz_r.at[i], (lax.rem(z + i, NZ), s)).start())

    back_block(64)

    def got_y(i):
        slot = a1.at[lax.rem(z + NZ - i, NZ)]
        remote(slot, slot, y_s.at[i], y_r.at[i], sibling).wait_recv()

    loop(1, NZ, got_y)
    for h in range(CH):
        top = jnp.concatenate([a1[4 * h], a1[4 * h + 1]], axis=1)
        bottom = jnp.concatenate([a1[4 * h + 2], a1[4 * h + 3]], axis=1)
        fin[core, h, rows16(q), :] = jnp.concatenate([top, bottom], axis=0).astype(BF16)

    def piece(i):
        return fin.at[core, :, rows16(i), :]

    def send_q(k):
        return remote(piece(q), piece(q), q_s.at[k], q_r.at[k], (z, chip(k) * 2 + core))

    def send_f(k):
        return remote(piece(chip_back(k)), piece(chip_back(k)), f_s.at[k], f_r.at[k], sibling)

    loop(1, NQ, lambda k: send_q(k).start())
    send_f(jnp.int32(0)).start()

    back_block(128)
    halo_g = phase_b_wait(1, after)
    for hf in range(2):
        gext[hf, ROWS:, :] = halo_g[:, hf * 128:(hf + 1) * 128]
    back_block(192)

    @pl.when(core == 0)
    def _():
        def got(i):
            slot = rz.at[lax.rem(z + NZ - i, NZ)]
            remote(slot, slot, kz_s.at[i], kz_r.at[i], sibling).wait_recv()

        loop(1, NZ, got)
        acc = rz[0]
        for i in range(1, NZ):
            acc = acc + rz[i]
        kf[q] = acc * FACTOR
        loop(1, NSEQ, lambda i: remote(
            kf.at[q], kf.at[q], kf_s.at[i], kf_r.at[q], (z, lax.rem(s + i, NSEQ))).start())

    def forward(k):
        slot = piece(chip_back(k))
        remote(slot, slot, q_s.at[k], q_r.at[k], sibling).wait_recv()
        send_f(k).start()

    loop(1, NQ, forward)

    def got_kf(i):
        slot = lax.rem(q + i, NQ)
        remote(kf.at[slot], kf.at[slot], kf_s.at[0], kf_r.at[slot], sibling).wait_recv()

    loop(1, NQ, got_kf)

    @pl.when(core == 1)
    def _():
        got_kf(0)

    for hf in range(2):
        cols = slice(hf * 128, (hf + 1) * 128)
        taps = jnp.concatenate([kf[2 * r + hf] for r in range(8)], axis=0)
        gk_ref[:, cols] = taps[:K, :].astype(BF16)
        gg_ref[:, cols] = taps[K:K + 1, :].astype(BF16)

    def got_f(k):
        slot = fin.at[1 - core, :, rows16(chip_back(k)), :]
        remote(slot, slot, f_s.at[k], f_r.at[k], sibling).wait_recv()

    loop(0, NQ, got_f)
    stores = []
    for h in range(CH):
        cols = pl.ds(h * 256, 256)
        stores.append(pltpu.make_async_copy(fin.at[0, h], gd_hbm.at[cols, :], st_sem.at[h]))
        stores.append(pltpu.make_async_copy(fin.at[1, h], gu_hbm.at[:, cols], st_sem.at[CH + h]))
    for copy in stores:
        copy.start()

    for d, src in ((0, tail), (1, head)):
        for i in range(1, 4):
            remote(src, src, a_s.at[d, i], a_r.at[d, i], sibling).wait_send()
        for i in range(1, 8):
            remote(send_b.at[d, i], send_b.at[d, i], b_s.at[d, i], b_r.at[d, i], sibling).wait_send()
    for h in range(CH):
        remote(outbound.at[h], outbound.at[h], c_s.at[h], c_r.at[h], sibling).wait_send()

        def sent(k, h=h):
            slot = tsum.at[h, rows16(chip(k)), :]
            remote(slot, slot, p_s.at[h, k], p_r.at[h, k], sibling).wait_send()

        loop(1, NQ, sent)
    loop(1, NZ, lambda i: send_z(i).wait_send())
    loop(1, NZ, lambda i: send_y(i).wait_send())
    loop(1, NQ, lambda k: send_q(k).wait_send())
    loop(0, NQ, lambda k: send_f(k).wait_send())
    loop(1, NQ, lambda i: send_k(i).wait_send())

    @pl.when(core == 1)
    def _():
        send_k(0).wait_send()

    @pl.when(core == 0)
    def _():
        loop(1, NZ, lambda i: remote(
            rz.at[z], rz.at[z], kz_s.at[i], kz_r.at[i], sibling).wait_send())
        loop(1, NSEQ, lambda i: remote(
            kf.at[q], kf.at[q], kf_s.at[i], kf_r.at[q], sibling).wait_send())

    for copy in stores:
        copy.wait()


def per_device(inputs, cotangent, lengths, placed, conv_weight, norm_gain, up_weight, down_weight):
    vm = pl.BlockSpec(memory_space=pltpu.VMEM)
    sm = pl.BlockSpec(memory_space=pltpu.SMEM)
    hb = pl.BlockSpec(memory_space=pl.ANY)
    V, D = pltpu.VMEM, pltpu.SemaphoreType.DMA
    out, gin, gk, gg, gu, gd = pl.pallas_call(
        kernel,
        out_shape=(
            jax.ShapeDtypeStruct((ROWS, C), BF16),
            jax.ShapeDtypeStruct((ROWS, C), BF16),
            jax.ShapeDtypeStruct((K, C), BF16),
            jax.ShapeDtypeStruct((1, C), BF16),
            jax.ShapeDtypeStruct((C, HID), BF16),
            jax.ShapeDtypeStruct((HID, C), BF16),
        ),
        in_specs=[sm, sm, vm, vm, vm, vm, hb, hb],
        out_specs=(vm, vm, vm, vm, hb, hb),
        scratch_shapes=[
            V((C, HID), BF16), V((HID, C), BF16),
            V((4, HALO, C), BF16), V((4, HALO, C), BF16), V((2, 8, HALO, C), BF16),
            V((8, HALO, C), BF16), V((8, HALO, C), BF16),
            V((HALO, C), BF16),
            V((2, HALO + ROWS, 128), F32), V((2, ROWS + HALO, 128), F32),
            V((ROWS, 128), jnp.int32), V((ROWS, 128), jnp.int32),
            V((ROWS, C), F32), V((ROWS, 128), F32), V((ROWS, C), BF16),
            V((ROWS, C), F32), V((ROWS, C), F32),
            V((CH, 256, 256), F32), V((CH, 256, 256), BF16), V((CH, 256, 256), BF16), V((CH, 256, 256), BF16),
            V((CH, NQ, 16, 256), BF16),
            V((NZ, 8, 128), F32), V((NZ, 8, 128), F32), V((NZ, 8, 128), F32),
            V((2, CH, 256, 256), BF16),
            V((2, K, 8, 128), F32), V((NQ, 8, 128), F32), V((NSEQ, 8, 128), F32),
            V((NZ, 8, 128), F32), V((NQ, 8, 128), F32),
            D((2,)), D((2, 4)), D((2, 4)), D((2, 8)), D((2, 8)), D((CH,)), D((CH,)),
            D((CH, NQ)), D((CH, NQ)), D((NZ,)), D((NZ,)), D((NZ,)), D((NZ,)), D((NQ,)), D((NQ,)),
            D((NQ,)), D((NQ,)), D((NQ,)), D((NSEQ,)), D((NZ,)), D((NZ,)), D((NSEQ,)), D((NQ,)), D((2 * CH,)),
        ],
        compiler_params=pltpu.CompilerParams(
            collective_id=0, has_side_effects=True, vmem_limit_bytes=48 * 2**20
        ),
    )(
        lengths, placed, inputs.reshape(ROWS, C), cotangent.reshape(ROWS, C), conv_weight,
        norm_gain.reshape(1, C), up_weight, down_weight,
    )
    return (
        out.reshape(inputs.shape), gin.reshape(inputs.shape), gk, gg.reshape(C), gu, gd,
    )


def solution(mesh):
    tok = P("dp", "seq", None, None)
    return jax.shard_map(
        per_device,
        mesh=mesh,
        in_specs=(tok, tok, P("dp", None), P("dp", None), P(), P(), P(), P()),
        out_specs=(tok, tok, P(), P(), P(), P()),
        check_vma=False,
    )
```

```python
import math

import jax
import jax.numpy as jnp
from jax import lax
from jax.experimental import pallas as pl
from jax.experimental.pallas import tpu as pltpu
from jax.sharding import PartitionSpec as P

MESH = pl.DeviceIdType.MESH
F32 = jnp.float32
BF16 = jnp.bfloat16

EPS = 1e-05
C = 256
HID = 1024
K = 51
ROWS = 256
TRACES = 8
HALO = 64
BLK = 64
NZ, NSEQ, NQ = 16, 32, 16
VM_BYTES = 60 * 2**20
CH = 4
FACTOR = 1.0 / math.sqrt(NZ * NSEQ * ROWS)
GELU_C = math.sqrt(2.0 / math.pi)
GELU_A = 0.044715
FAR_Z = (8, 7, 9, 6, 10, 5, 11, 4, 12, 3, 13, 2, 14, 1, 15)


def dot(a, b, ca, cb):
    return lax.dot_general(a, b, (((ca,), (cb,)), ((), ())), preferred_element_type=F32)


def remote(src, dst, send, recv, dev):
    return pltpu.make_async_remote_copy(
        src_ref=src, dst_ref=dst, send_sem=send, recv_sem=recv, device_id=dev, device_id_type=MESH
    )


def loop(lo, hi, body):
    def step(i, carry):
        body(i)
        return carry

    lax.fori_loop(lo, hi, step, 0)


def kernel(
    lengths, placed, x_hbm, dy_hbm, w_hbm, gain_hbm, up_hbm, down_hbm,
    out_hbm, gin_hbm, gk_hbm, gg_hbm, gu_hbm, gd_hbm,
    out_ref, gin_ref, gk_ref, gg_ref, fin, x_ref, dy_ref, w_ref, gain_ref, up_v, down_v,
    gath0, gath1, send_b, recv0, recv1, head, ext, gext, dep, rem_, normed_s, istd_s, scaled_s,
    gn_s, oacc_s, own, other, outbound, sib, tsum, r1, zs, r2, a1, kp, gp, kb, rk, rz, kf,
    ld_sem, a_s, a_r, b_s, b_r, c_s, c_r, p_s, p_r, z_s, z_r, y_s, y_r, q_s, q_r, f_s, f_r,
    k_s, k_r, kz_s, kz_r, kf_s, kf_r, st_sem,
):
    z = lax.axis_index("dp")
    s = lax.axis_index("seq")
    core = lax.rem(s, 2)
    q = lax.div(s, 2)
    yy = lax.rem(q, 4)
    xx = lax.div(q, 4)
    g = xx * 2 + core
    gz = lax.div(z, 4)
    sibling = (z, q * 2 + 1 - core)
    gath, recv = (gath0, gath1), (recv0, recv1)

    bar = pltpu.get_barrier_semaphore()
    for i in FAR_Z:
        pl.semaphore_signal(bar, inc=1, device_id=(lax.rem(z + i, NZ), s), device_id_type=MESH)
    loop(0, NSEQ - 1, lambda i: pl.semaphore_signal(
        bar, inc=1, device_id=(z, lax.rem(s + 1 + lax.rem(i + 19, NSEQ - 1), NSEQ)), device_id_type=MESH))
    loads = [
        pltpu.make_async_copy(src, dst, ld_sem.at[i])
        for i, (src, dst) in enumerate((
            (x_hbm, x_ref), (w_hbm, w_ref), (gain_hbm, gain_ref),
            (dy_hbm, dy_ref), (up_hbm, up_v), (down_hbm, down_v)))
    ]
    for copy in loads:
        copy.start()

    def target(i):
        gt = lax.rem(g + i, 8)
        return (lax.div(gt, 2) * 4 + yy) * 2 + lax.rem(gt, 2)

    targets = [target(i) for i in range(8)]
    at = [placed[0, t] for t in targets]

    def look(k, found):
        p = placed[0, k]
        return tuple(
            jnp.where(p == at[i % 8] + (-1 if i < 8 else 1), k, f) for i, f in enumerate(found)
        )

    found = lax.fori_loop(0, NSEQ, look, (jnp.int32(0),) * 16)
    before, after = found[:8], found[8:]

    def y_of(slot):
        return lax.rem(lax.div(slot, 2), 4)

    def g_of(slot):
        return lax.div(slot, 8) * 2 + lax.rem(slot, 2)

    pos = at[0] * ROWS + lax.broadcasted_iota(jnp.int32, (ROWS, 128), 0)
    ends, end = [], jnp.int32(0)
    for i in range(TRACES):
        end = end + lengths[0, i]
        ends.append(end)
    start = jnp.zeros((ROWS, 128), jnp.int32)
    for e in ends:
        start = jnp.where(e <= pos, e, start)
    dep[...] = pos - start
    stop = jnp.zeros((ROWS, 128), jnp.int32)
    for e in reversed(ends):
        stop = jnp.where(e > pos, e, stop)
    rem_[...] = stop - 1 - pos
    loads[0].wait()
    for hf in range(2):
        ext[hf, HALO:, :] = x_ref[:, hf * 128:(hf + 1) * 128].astype(F32)
    loads[1].wait()
    loads[2].wait()

    def phase_a(d, src):
        for i in range(1, 4):
            peer = (xx * 4 + lax.rem(yy + i, 4)) * 2 + core
            remote(src, gath[d].at[yy], a_s.at[d, i], a_r.at[d, i], (z, peer)).start()
        gath[d][yy] = src[...]

    def phase_a_wait(d):
        for i in range(1, 4):
            slot = gath[d].at[lax.rem(yy + 4 - i, 4)]
            remote(slot, slot, a_s.at[d, i], a_r.at[d, i], sibling).wait_recv()

    def phase_b(d, source):
        for i in (4, 5, 3, 2, 6, 7, 1):
            send_b[d, i] = gath[d][y_of(source[i])]
            remote(send_b.at[d, i], recv[d].at[g], b_s.at[d, i], b_r.at[d, i], (z, targets[i])).start()
        recv[d][g] = gath[d][y_of(source[0])]

    def phase_b_wait(d, source):
        for i in range(1, 8):
            slot = recv[d].at[lax.rem(g + 8 - i, 8)]
            remote(slot, slot, b_s.at[d, i], b_r.at[d, i], sibling).wait_recv()
        return recv[d][g_of(source[0])].astype(F32)

    pl.semaphore_wait(bar, NSEQ - 1 + NZ - 1)
    tail = x_ref.at[pl.ds(ROWS - HALO, HALO), :]
    phase_a(0, tail)

    def depthwise(src, base, sign, mask_ref, r0):
        m = mask_ref[r0:r0 + BLK, :]
        acc = [jnp.zeros((BLK, 128), F32) for _ in range(2)]
        for j in range(K):
            lo = base + r0 + sign * j
            inside = m >= j
            for hf in range(2):
                win = src[hf, lo:lo + BLK, :] * w_ref[j:j + 1, hf * 128:(hf + 1) * 128]
                acc[hf] = acc[hf] + jnp.where(inside, win, 0.0)
        return acc

    def forward_block(r0):
        a0, a1_ = depthwise(ext, HALO, -1, dep, r0)
        mean = jnp.sum(a0 + a1_, axis=1, keepdims=True) * (1.0 / C)
        a0, a1_ = a0 - mean, a1_ - mean
        var = jnp.sum(a0 * a0 + a1_ * a1_, axis=1, keepdims=True) * (1.0 / C)
        inv = lax.rsqrt(var + EPS)
        istd_s[r0:r0 + BLK, :] = jnp.broadcast_to(inv, (BLK, 128))
        for hf, a in enumerate((a0, a1_)):
            cols = slice(hf * 128, (hf + 1) * 128)
            n = a * inv
            normed_s[r0:r0 + BLK, cols] = n
            scaled_s[r0:r0 + BLK, cols] = (n * gain_ref[0:1, cols]).astype(BF16)

    def rows16(i):
        return pl.ds(pl.multiple_of(i * 16, 16), 16)

    def offset(k):
        return 1 + lax.rem(k + 9, NQ - 1)

    def chip(k):
        return lax.rem(xx + lax.div(k, 4), 4) * 4 + lax.rem(yy + lax.rem(k, 4), 4)

    order = [lax.rem(gz + i, CH) for i in (2, 1, 3, 0)]

    def feed_forward(o, r0, r1_):
        cols = pl.ds(pl.multiple_of(order[o] * 256, 256), 256)
        up_c = up_v[:, cols]
        down_c = down_v[cols, :]
        sc = scaled_s[r0:r1_, :]
        dy = dy_ref[r0:r1_, :]
        hid = dot(sc, up_c, 1, 0)
        gact = dot(dy, down_c, 1, 1)
        h2 = hid * hid
        th = jnp.tanh(hid * (GELU_C + (GELU_C * GELU_A) * h2))
        h1 = 0.5 + 0.5 * th
        act = hid * h1
        slope = h1 + act * (1.0 - th) * (GELU_C + (3.0 * GELU_C * GELU_A) * h2)
        act = act.astype(BF16)
        gh = (gact * slope).astype(BF16)
        out = dot(act, down_c, 1, 0)
        n = dot(gh, up_c, 1, 1)
        if o == 0:
            oacc_s[r0:r1_, :] = out
            gn_s[r0:r1_, :] = n
        else:
            oacc_s[r0:r1_, :] += out
            gn_s[r0:r1_, :] += n
        gdown = dot(act, dy, 0, 0)
        gup = dot(sc, gh, 0, 0)
        first = core == 0
        mine, theirs = jnp.where(first, gdown, gup), jnp.where(first, gup, gdown)
        if r0:
            own[o] = mine
            other[o] = theirs
        else:
            own[o] += mine
            outbound[o] = (other[o] + theirs).astype(BF16)
            remote(outbound.at[o], sib.at[o], c_s.at[o], c_r.at[o], sibling).start()

    def pair_stage(o):
        remote(sib.at[o], sib.at[o], c_s.at[o], c_r.at[o], sibling).wait_recv()
        tsum[o] = (own[o] + sib[o].astype(F32)).astype(BF16)

        def send(i):
            k = offset(i)
            qp = chip(k)
            remote(tsum.at[o, rows16(qp), :], r1.at[o, k], p_s.at[o, k], p_r.at[o, k],
                   (z, qp * 2 + core)).start()

        loop(0, NQ - 1, send)

    def norm_back(r0):
        gn = gn_s[r0:r0 + BLK, :]
        nm = normed_s[r0:r0 + BLK, :]
        prod = gn * nm
        part = jnp.sum(prod.reshape(BLK // 8, 8, C), axis=0)
        if r0 == BLK:
            gp[...] = part
        else:
            gp[...] += part
        qv = gn * gain_ref[...]
        qn = prod * gain_ref[...]
        m1 = jnp.sum(qv[:, :128] + qv[:, 128:], axis=1, keepdims=True) * (1.0 / C)
        m2 = jnp.sum(qn[:, :128] + qn[:, 128:], axis=1, keepdims=True) * (1.0 / C)
        t = qv - m1 - nm * m2
        for hf in range(2):
            gext[hf, r0:r0 + BLK, :] = t[:, hf * 128:(hf + 1) * 128] * istd_s[r0:r0 + BLK, :]

    def tap_block(r0):
        m = dep[r0:r0 + BLK, :]
        gc = [gext[hf, r0:r0 + BLK, :] for hf in range(2)]
        for j in range(K):
            lo = HALO + r0 - j
            inside = m >= j
            for hf in range(2):
                v = jnp.where(inside, gc[hf] * ext[hf, lo:lo + BLK, :], 0.0)
                part = jnp.sum(v.reshape(BLK // 8, 8, 128), axis=0)
                if r0 == BLK:
                    kp[hf, j] = part
                else:
                    kp[hf, j] += part

    def back_block(r0):
        acc = depthwise(gext, 0, 1, rem_, r0)
        for hf in range(2):
            cols = slice(hf * 128, (hf + 1) * 128)
            gin_ref[r0:r0 + BLK, cols] = (dy_ref[r0:r0 + BLK, cols].astype(F32) + acc[hf]).astype(BF16)

    later = range(BLK, ROWS, BLK)
    for r0 in later:
        forward_block(r0)
    for copy in loads[3:]:
        copy.wait()
    feed_forward(0, BLK, ROWS)
    phase_a_wait(0)
    phase_b(0, before)
    for o in range(1, CH):
        feed_forward(o, BLK, ROWS)
    for r0 in later:
        norm_back(r0)
    for r0 in later:
        tap_block(r0)

    halo = phase_b_wait(0, before)
    for hf in range(2):
        ext[hf, :HALO, :] = halo[:, hf * 128:(hf + 1) * 128]
    forward_block(0)
    for o in range(CH):
        feed_forward(o, 0, BLK)
        if o:
            pair_stage(o - 1)
    pair_stage(CH - 1)
    norm_back(0)
    for hf in range(2):
        head[:, hf * 128:(hf + 1) * 128] = gext[hf, :HALO, :].astype(BF16)
    phase_a(1, head)
    tap_block(0)
    for hf in range(2):
        taps = jnp.sum(kp[hf], axis=1)
        gain = jnp.sum(gp[:, hf * 128:(hf + 1) * 128], axis=0, keepdims=True)
        taps = jnp.concatenate([taps, gain, jnp.zeros((64 - K - 1, 128), F32)], axis=0)
        for r in range(8):
            kb[2 * r + hf] = taps[r * 8:r * 8 + 8, :]

    def send_k(i):
        p = lax.rem(q + i, NQ)
        return remote(kb.at[p], rk.at[s], k_s.at[i], k_r.at[s], (z, p * 2))

    def send_z(zp):
        return remote(zs.at[zp], r2.at[z], z_s.at[zp], z_r.at[z], (zp, s))

    def plane_sum(o):
        def got(k):
            remote(r1.at[o, k], r1.at[o, k], p_s.at[o, k], p_r.at[o, k], sibling).wait_recv()

        loop(1, NQ, got)
        acc = tsum[o, rows16(q), :].astype(F32)
        for k in range(1, NQ):
            acc = acc + r1[o, k].astype(F32)
        for j in range(4):
            rh, hf = j // 2, j % 2
            zs[order[o] * 4 + j] = acc[rh * 8:rh * 8 + 8, hf * 128:(hf + 1) * 128]
        for j in range(4):
            zp = order[o] * 4 + j

            @pl.when(zp != z)
            def _(zp=zp):
                send_z(zp).start()

    for o in range(CH):
        plane_sum(o)

    loop(1, NQ, lambda i: send_k(i).start())

    @pl.when(core == 1)
    def _():
        send_k(0).start()

    phase_a_wait(1)
    phase_b(1, after)
    out_ref[...] = (x_ref[...].astype(F32) + oacc_s[...]).astype(BF16)
    back_block(BLK)

    def got_z(i):
        zp = lax.rem(z + i, NZ)
        remote(r2.at[zp], r2.at[zp], z_s.at[zp], z_r.at[zp], sibling).wait_recv()

    loop(1, NZ, got_z)
    total = zs[z]
    for i in range(1, NZ):
        total = total + r2[lax.rem(z + i, NZ)]
    a1[z] = total * FACTOR

    def send_y(i):
        return remote(a1.at[z], a1.at[z], y_s.at[i], y_r.at[z], (lax.rem(z + i, NZ), s))

    for i in FAR_Z:
        send_y(i).start()

    @pl.when(core == 0)
    def _():
        def got(i):
            sp = lax.rem(s + i, NSEQ)
            remote(rk.at[sp], rk.at[sp], k_s.at[0], k_r.at[sp], sibling).wait_recv()

        loop(1, NSEQ, got)
        rk[s] = kb[q]
        acc = rk[0]
        for i in range(1, NSEQ):
            acc = acc + rk[i]
        rz[z] = acc
        loop(1, NZ, lambda i: remote(
            rz.at[z], rz.at[z], kz_s.at[i], kz_r.at[i], (lax.rem(z + i, NZ), s)).start())

    back_block(0)
    back_block(2 * BLK)

    def chunk_of(o):
        return lax.rem(gz + (0, 1, 3, 2)[o], CH)

    def send_q(o, k):
        piece = fin.at[core, chunk_of(o), rows16(q), :]
        return remote(piece, piece, q_s.at[o, k], q_r.at[o, k], (z, chip(k) * 2 + core))

    for o in range(CH):
        h = chunk_of(o)
        for j in range(4):
            zp = h * 4 + j

            @pl.when(zp != z)
            def _(zp=zp):
                remote(a1.at[zp], a1.at[zp], y_s.at[0], y_r.at[zp], sibling).wait_recv()

        top = jnp.concatenate([a1[4 * h], a1[4 * h + 1]], axis=1)
        bottom = jnp.concatenate([a1[4 * h + 2], a1[4 * h + 3]], axis=1)
        fin[core, h, rows16(q), :] = jnp.concatenate([top, bottom], axis=0).astype(BF16)
        loop(0, NQ - 1, lambda i, o=o: send_q(o, offset(i)).start())

    halo_g = phase_b_wait(1, after)
    for hf in range(2):
        gext[hf, ROWS:, :] = halo_g[:, hf * 128:(hf + 1) * 128]
    back_block(3 * BLK)
    stores = [
        pltpu.make_async_copy(src, dst, st_sem.at[i])
        for i, (src, dst) in enumerate((
            (out_ref, out_hbm), (gin_ref, gin_hbm), (gk_ref, gk_hbm), (gg_ref, gg_hbm)))
    ]
    stores[0].start()
    stores[1].start()

    @pl.when(core == 0)
    def _():
        def got(i):
            slot = rz.at[lax.rem(z + NZ - i, NZ)]
            remote(slot, slot, kz_s.at[i], kz_r.at[i], sibling).wait_recv()

        loop(1, NZ, got)
        acc = rz[0]
        for i in range(1, NZ):
            acc = acc + rz[i]
        kf[q] = acc * FACTOR
        loop(1, NSEQ, lambda i: remote(
            kf.at[q], kf.at[q], kf_s.at[i], kf_r.at[q], (z, lax.rem(s + i, NSEQ))).start())

    def send_f(o):
        half = fin.at[core, chunk_of(o)]
        return remote(half, half, f_s.at[o], f_r.at[o], sibling)

    def store(matrix, o):
        part = pl.ds(pl.multiple_of(chunk_of(o) * 256, 256), 256)

        @pl.when(matrix == 0)
        def _():
            pltpu.make_async_copy(fin.at[0, chunk_of(o)], gd_hbm.at[part, :], st_sem.at[4 + o]).start()

        @pl.when(matrix == 1)
        def _():
            pltpu.make_async_copy(fin.at[1, chunk_of(o)], gu_hbm.at[:, part], st_sem.at[8 + o]).start()

    for o in range(CH):
        def got_q(k, o=o):
            qs = lax.rem(xx + 4 - lax.div(k, 4), 4) * 4 + lax.rem(yy + 4 - lax.rem(k, 4), 4)
            piece = fin.at[core, chunk_of(o), rows16(qs), :]
            remote(piece, piece, q_s.at[o, k], q_r.at[o, k], sibling).wait_recv()

        loop(1, NQ, got_q)
        send_f(o).start()
        store(core, o)

    def got_kf(i):
        slot = lax.rem(q + i, NQ)
        remote(kf.at[slot], kf.at[slot], kf_s.at[0], kf_r.at[slot], sibling).wait_recv()

    loop(1, NQ, got_kf)

    @pl.when(core == 1)
    def _():
        got_kf(0)

    for hf in range(2):
        cols = slice(hf * 128, (hf + 1) * 128)
        taps = jnp.concatenate([kf[2 * r + hf] for r in range(8)], axis=0)
        gk_ref[:, cols] = taps[:K, :].astype(BF16)
        gg_ref[:, cols] = taps[K:K + 1, :]
    stores[2].start()
    stores[3].start()
    for o in range(CH):
        half = fin.at[1 - core, chunk_of(o)]
        remote(half, half, f_s.at[o], f_r.at[o], sibling).wait_recv()
        store(1 - core, o)

    for d, src in ((0, tail), (1, head)):
        for i in range(1, 4):
            remote(src, src, a_s.at[d, i], a_r.at[d, i], sibling).wait_send()
        for i in range(1, 8):
            remote(send_b.at[d, i], send_b.at[d, i], b_s.at[d, i], b_r.at[d, i], sibling).wait_send()
    for o in range(CH):
        remote(outbound.at[o], outbound.at[o], c_s.at[o], c_r.at[o], sibling).wait_send()

        def sent(k, o=o):
            slot = tsum.at[o, rows16(chip(k)), :]
            remote(slot, slot, p_s.at[o, k], p_r.at[o, k], sibling).wait_send()
            send_q(o, k).wait_send()

        loop(1, NQ, sent)
        send_f(o).wait_send()
    loop(1, NZ, lambda i: send_z(lax.rem(z + i, NZ)).wait_send())
    loop(1, NZ, lambda i: send_y(i).wait_send())
    loop(1, NQ, lambda i: send_k(i).wait_send())

    @pl.when(core == 1)
    def _():
        send_k(0).wait_send()

    @pl.when(core == 0)
    def _():
        loop(1, NZ, lambda i: remote(
            rz.at[z], rz.at[z], kz_s.at[i], kz_r.at[i], sibling).wait_send())
        loop(1, NSEQ, lambda i: remote(
            kf.at[q], kf.at[q], kf_s.at[i], kf_r.at[q], sibling).wait_send())

    for copy in stores:
        copy.wait()
    for o in range(CH):
        part = pl.ds(pl.multiple_of(chunk_of(o) * 256, 256), 256)
        pltpu.make_async_copy(fin.at[0, chunk_of(o)], gd_hbm.at[part, :], st_sem.at[4 + o]).wait()
        pltpu.make_async_copy(fin.at[1, chunk_of(o)], gu_hbm.at[:, part], st_sem.at[8 + o]).wait()


def finish(out_i, gin_i, gk_i, gu_i, gd_i, gg_i, out_o, gin_o, gk_o, gu_o, gd_o, gg_o, sem):
    pairs = ((out_i, out_o), (gin_i, gin_o), (gk_i, gk_o), (gu_i, gu_o), (gd_i, gd_o))
    copies = [pltpu.make_async_copy(a, b, sem.at[i]) for i, (a, b) in enumerate(pairs)]
    for copy in copies:
        copy.start()
    gg_o[...] = gg_i[0, :].astype(BF16)
    for copy in copies:
        copy.wait()


def per_device(inputs, cotangent, lengths, placed, conv_weight, norm_gain, up_weight, down_weight):
    vm = pl.BlockSpec(memory_space=pltpu.VMEM)
    sm = pl.BlockSpec(memory_space=pltpu.SMEM)
    hb = pl.BlockSpec(memory_space=pltpu.HBM)
    V, D = pltpu.VMEM, pltpu.SemaphoreType.DMA
    out, gin, gk, gg, gu, gd = pl.pallas_call(
        kernel,
        out_shape=(
            jax.ShapeDtypeStruct((ROWS, C), BF16),
            jax.ShapeDtypeStruct((ROWS, C), BF16),
            jax.ShapeDtypeStruct((K, C), BF16),
            jax.ShapeDtypeStruct((1, C), F32),
            jax.ShapeDtypeStruct((C, HID), BF16),
            jax.ShapeDtypeStruct((HID, C), BF16),
        ),
        in_specs=[sm, sm, hb, hb, hb, hb, hb, hb],
        out_specs=(hb,) * 6,
        scratch_shapes=[
            V((ROWS, C), BF16), V((ROWS, C), BF16), V((K, C), BF16), V((1, C), F32),
            V((2, CH, 256, 256), BF16),
            V((ROWS, C), BF16), V((ROWS, C), BF16), V((K, C), F32), V((1, C), F32),
            V((C, HID), BF16), V((HID, C), BF16),
            V((4, HALO, C), BF16), V((4, HALO, C), BF16), V((2, 8, HALO, C), BF16),
            V((8, HALO, C), BF16), V((8, HALO, C), BF16),
            V((HALO, C), BF16),
            V((2, HALO + ROWS, 128), F32), V((2, ROWS + HALO, 128), F32),
            V((ROWS, 128), jnp.int32), V((ROWS, 128), jnp.int32),
            V((ROWS, C), F32), V((ROWS, 128), F32), V((ROWS, C), BF16),
            V((ROWS, C), F32), V((ROWS, C), F32),
            V((CH, 256, 256), F32), V((CH, 256, 256), F32),
            V((CH, 256, 256), BF16), V((CH, 256, 256), BF16), V((CH, 256, 256), BF16),
            V((CH, NQ, 16, 256), BF16),
            V((NZ, 8, 128), F32), V((NZ, 8, 128), F32), V((NZ, 8, 128), F32),
            V((2, K, 8, 128), F32), V((8, C), F32), V((NQ, 8, 128), F32), V((NSEQ, 8, 128), F32),
            V((NZ, 8, 128), F32), V((NQ, 8, 128), F32),
            D((6,)), D((2, 4)), D((2, 4)), D((2, 8)), D((2, 8)), D((CH,)), D((CH,)),
            D((CH, NQ)), D((CH, NQ)), D((NZ,)), D((NZ,)), D((NZ,)), D((NZ,)), D((CH, NQ)), D((CH, NQ)),
            D((CH,)), D((CH,)), D((NQ,)), D((NSEQ,)), D((NZ,)), D((NZ,)), D((NSEQ,)), D((NQ,)), D((12,)),
        ],
        compiler_params=pltpu.CompilerParams(
            collective_id=0, has_side_effects=True, vmem_limit_bytes=VM_BYTES
        ),
    )(
        lengths, placed, inputs.reshape(ROWS, C), cotangent.reshape(ROWS, C), conv_weight,
        norm_gain.reshape(1, C), up_weight, down_weight,
    )
    out, gin, gk, gu, gd, gg = pl.pallas_call(
        finish,
        out_shape=(
            jax.ShapeDtypeStruct((ROWS, C), BF16),
            jax.ShapeDtypeStruct((ROWS, C), BF16),
            jax.ShapeDtypeStruct((K, C), BF16),
            jax.ShapeDtypeStruct((C, HID), BF16),
            jax.ShapeDtypeStruct((HID, C), BF16),
            jax.ShapeDtypeStruct((C,), BF16),
        ),
        in_specs=[hb, hb, hb, hb, hb, vm],
        out_specs=(hb, hb, hb, hb, hb, vm),
        scratch_shapes=[D((5,))],
    )(out, gin, gk, gu, gd, gg)
    return (
        out.reshape(inputs.shape), gin.reshape(inputs.shape), gk, gg, gu, gd,
    )


def solution(mesh):
    tok = P("dp", "seq", None, None)
    return jax.shard_map(
        per_device,
        mesh=mesh,
        in_specs=(tok, tok, P("dp", None), P("dp", None), P(), P(), P(), P()),
        out_specs=(tok, tok, P(), P(), P(), P()),
        check_vma=False,
    )
```

```python
import math

import jax
import jax.numpy as jnp
from jax import lax
from jax.experimental import pallas as pl
from jax.experimental.pallas import tpu as pltpu
from jax.sharding import PartitionSpec as P

MESH = pl.DeviceIdType.MESH
F32 = jnp.float32
BF16 = jnp.bfloat16

EPS = 1e-05
C = 256
HID = 1024
K = 51
ROWS = 256
TRACES = 8
HALO = 64
BLK = 64
NZ, NSEQ, NQ = 16, 32, 16
VM_BYTES = 60 * 2**20
CH = 4
FACTOR = 1.0 / math.sqrt(NZ * NSEQ * ROWS)
GELU_C = math.sqrt(2.0 / math.pi)
GELU_A = 0.044715
FAR_Z = (8, 7, 9, 6, 10, 5, 11, 4, 12, 3, 13, 2, 14, 1, 15)


def dot(a, b, ca, cb):
    return lax.dot_general(a, b, (((ca,), (cb,)), ((), ())), preferred_element_type=F32)


def remote(src, dst, send, recv, dev):
    return pltpu.make_async_remote_copy(
        src_ref=src, dst_ref=dst, send_sem=send, recv_sem=recv, device_id=dev, device_id_type=MESH
    )


def loop(lo, hi, body):
    def step(i, carry):
        body(i)
        return carry

    lax.fori_loop(lo, hi, step, 0)


def kernel(
    lengths, placed, x_hbm, dy_hbm, w_hbm, gain_hbm, up_hbm, down_hbm,
    out_hbm, gin_hbm, gk_hbm, gg_hbm, gu_hbm, gd_hbm,
    out_ref, gin_ref, gk_ref, gg_ref, fin, x_ref, dy_ref, w_ref, gain_ref, up_v, down_v,
    gath0, gath1, send_b, recv0, recv1, head, ext, gext, dep, rem_, normed_s, istd_s, scaled_s,
    gn_s, oacc_s, own, other, outbound, sib, tsum, r1, zs, r2, a1, kp, gp, kb, rk, rz, kf,
    ld_sem, a_s, a_r, b_s, b_r, c_s, c_r, p_s, p_r, z_s, z_r, y_s, y_r, q_s, q_r, f_s, f_r,
    k_s, k_r, kz_s, kz_r, kf_s, kf_r, st_sem,
):
    z = lax.axis_index("dp")
    s = lax.axis_index("seq")
    core = lax.rem(s, 2)
    q = lax.div(s, 2)
    yy = lax.rem(q, 4)
    xx = lax.div(q, 4)
    g = xx * 2 + core
    gz = lax.div(z, 4)
    sibling = (z, q * 2 + 1 - core)
    gath, recv = (gath0, gath1), (recv0, recv1)

    bar = pltpu.get_barrier_semaphore()
    for i in FAR_Z:
        pl.semaphore_signal(bar, inc=1, device_id=(lax.rem(z + i, NZ), s), device_id_type=MESH)
    loop(0, NSEQ - 1, lambda i: pl.semaphore_signal(
        bar, inc=1, device_id=(z, lax.rem(s + 1 + lax.rem(i + 19, NSEQ - 1), NSEQ)), device_id_type=MESH))
    loads = [
        pltpu.make_async_copy(src, dst, ld_sem.at[i])
        for i, (src, dst) in enumerate((
            (x_hbm, x_ref), (w_hbm, w_ref), (gain_hbm, gain_ref),
            (dy_hbm, dy_ref), (up_hbm, up_v), (down_hbm, down_v)))
    ]
    for copy in loads:
        copy.start()

    def target(i):
        gt = lax.rem(g + i, 8)
        return (lax.div(gt, 2) * 4 + yy) * 2 + lax.rem(gt, 2)

    targets = [target(i) for i in range(8)]
    at = [placed[0, t] for t in targets]

    def look(k, found):
        p = placed[0, k]
        return tuple(
            jnp.where(p == at[i % 8] + (-1 if i < 8 else 1), k, f) for i, f in enumerate(found)
        )

    found = lax.fori_loop(0, NSEQ, look, (jnp.int32(0),) * 16)
    before, after = found[:8], found[8:]

    def y_of(slot):
        return lax.rem(lax.div(slot, 2), 4)

    def g_of(slot):
        return lax.div(slot, 8) * 2 + lax.rem(slot, 2)

    pos = at[0] * ROWS + lax.broadcasted_iota(jnp.int32, (ROWS, 128), 0)
    ends, end = [], jnp.int32(0)
    for i in range(TRACES):
        end = end + lengths[0, i]
        ends.append(end)
    start = jnp.zeros((ROWS, 128), jnp.int32)
    for e in ends:
        start = jnp.where(e <= pos, e, start)
    dep[...] = pos - start
    stop = jnp.zeros((ROWS, 128), jnp.int32)
    for e in reversed(ends):
        stop = jnp.where(e > pos, e, stop)
    rem_[...] = stop - 1 - pos
    loads[0].wait()
    for hf in range(2):
        ext[hf, HALO:, :] = x_ref[:, hf * 128:(hf + 1) * 128].astype(F32)
    loads[1].wait()
    loads[2].wait()

    def phase_a(d, src):
        for i in range(1, 4):
            peer = (xx * 4 + lax.rem(yy + i, 4)) * 2 + core
            remote(src, gath[d].at[yy], a_s.at[d, i], a_r.at[d, i], (z, peer)).start()
        gath[d][yy] = src[...]

    def phase_a_wait(d):
        for i in range(1, 4):
            slot = gath[d].at[lax.rem(yy + 4 - i, 4)]
            remote(slot, slot, a_s.at[d, i], a_r.at[d, i], sibling).wait_recv()

    def phase_b(d, source):
        for i in (4, 5, 3, 2, 6, 7, 1):
            send_b[d, i] = gath[d][y_of(source[i])]
            remote(send_b.at[d, i], recv[d].at[g], b_s.at[d, i], b_r.at[d, i], (z, targets[i])).start()
        recv[d][g] = gath[d][y_of(source[0])]

    def phase_b_wait(d, source):
        for i in range(1, 8):
            slot = recv[d].at[lax.rem(g + 8 - i, 8)]
            remote(slot, slot, b_s.at[d, i], b_r.at[d, i], sibling).wait_recv()
        return recv[d][g_of(source[0])].astype(F32)

    pl.semaphore_wait(bar, NSEQ - 1 + NZ - 1)
    tail = x_ref.at[pl.ds(ROWS - HALO, HALO), :]
    phase_a(0, tail)

    def depthwise(src, base, sign, mask_ref, r0):
        m = mask_ref[r0:r0 + BLK, :]
        acc = [jnp.zeros((BLK, 128), F32) for _ in range(2)]
        for j in range(K):
            lo = base + r0 + sign * j
            inside = m >= j
            for hf in range(2):
                win = src[hf, lo:lo + BLK, :] * w_ref[j:j + 1, hf * 128:(hf + 1) * 128]
                acc[hf] = acc[hf] + jnp.where(inside, win, 0.0)
        return acc

    def forward_block(r0):
        a0, a1_ = depthwise(ext, HALO, -1, dep, r0)
        mean = jnp.sum(a0 + a1_, axis=1, keepdims=True) * (1.0 / C)
        a0, a1_ = a0 - mean, a1_ - mean
        var = jnp.sum(a0 * a0 + a1_ * a1_, axis=1, keepdims=True) * (1.0 / C)
        inv = lax.rsqrt(var + EPS)
        istd_s[r0:r0 + BLK, :] = jnp.broadcast_to(inv, (BLK, 128))
        for hf, a in enumerate((a0, a1_)):
            cols = slice(hf * 128, (hf + 1) * 128)
            n = a * inv
            normed_s[r0:r0 + BLK, cols] = n
            scaled_s[r0:r0 + BLK, cols] = (n * gain_ref[0:1, cols]).astype(BF16)

    def rows16(i):
        return pl.ds(pl.multiple_of(i * 16, 16), 16)

    def offset(k):
        return 1 + lax.rem(k + 9, NQ - 1)

    def chip(k):
        return lax.rem(xx + lax.div(k, 4), 4) * 4 + lax.rem(yy + lax.rem(k, 4), 4)

    order = [lax.rem(gz + i, CH) for i in (2, 1, 3, 0)]

    def feed_forward(o, r0, r1_):
        cols = pl.ds(pl.multiple_of(order[o] * 256, 256), 256)
        up_c = up_v[:, cols]
        down_c = down_v[cols, :]
        sc = scaled_s[r0:r1_, :]
        dy = dy_ref[r0:r1_, :]
        hid = dot(sc, up_c, 1, 0)
        gact = dot(dy, down_c, 1, 1)
        h2 = hid * hid
        th = jnp.tanh(hid * (GELU_C + (GELU_C * GELU_A) * h2))
        h1 = 0.5 + 0.5 * th
        act = hid * h1
        slope = h1 + act * (1.0 - th) * (GELU_C + (3.0 * GELU_C * GELU_A) * h2)
        act = act.astype(BF16)
        gh = (gact * slope).astype(BF16)
        out = dot(act, down_c, 1, 0)
        n = dot(gh, up_c, 1, 1)
        if o == 0:
            oacc_s[r0:r1_, :] = out
            gn_s[r0:r1_, :] = n
        else:
            oacc_s[r0:r1_, :] += out
            gn_s[r0:r1_, :] += n
        gdown = dot(act, dy, 0, 0)
        gup = dot(sc, gh, 0, 0)
        first = core == 0
        mine, theirs = jnp.where(first, gdown, gup), jnp.where(first, gup, gdown)
        if r0:
            own[o] = mine
            other[o] = theirs
        else:
            own[o] += mine
            outbound[o] = (other[o] + theirs).astype(BF16)
            remote(outbound.at[o], sib.at[o], c_s.at[o], c_r.at[o], sibling).start()

    def pair_stage(o):
        remote(sib.at[o], sib.at[o], c_s.at[o], c_r.at[o], sibling).wait_recv()
        tsum[o] = (own[o] + sib[o].astype(F32)).astype(BF16)

        def send(i):
            k = offset(i)
            qp = chip(k)
            remote(tsum.at[o, rows16(qp), :], r1.at[o, k], p_s.at[o, k], p_r.at[o, k],
                   (z, qp * 2 + core)).start()

        loop(0, NQ - 1, send)

    def norm_back(r0):
        gn = gn_s[r0:r0 + BLK, :]
        nm = normed_s[r0:r0 + BLK, :]
        prod = gn * nm
        part = jnp.sum(prod.reshape(BLK // 8, 8, C), axis=0)
        if r0 == BLK:
            gp[...] = part
        else:
            gp[...] += part
        qv = gn * gain_ref[...]
        qn = prod * gain_ref[...]
        m1 = jnp.sum(qv[:, :128] + qv[:, 128:], axis=1, keepdims=True) * (1.0 / C)
        m2 = jnp.sum(qn[:, :128] + qn[:, 128:], axis=1, keepdims=True) * (1.0 / C)
        t = qv - m1 - nm * m2
        for hf in range(2):
            gext[hf, r0:r0 + BLK, :] = t[:, hf * 128:(hf + 1) * 128] * istd_s[r0:r0 + BLK, :]

    def tap_block(r0):
        m = dep[r0:r0 + BLK, :]
        gc = [gext[hf, r0:r0 + BLK, :] for hf in range(2)]
        for j in range(K):
            lo = HALO + r0 - j
            inside = m >= j
            for hf in range(2):
                v = jnp.where(inside, gc[hf] * ext[hf, lo:lo + BLK, :], 0.0)
                part = jnp.sum(v.reshape(BLK // 8, 8, 128), axis=0)
                if r0 == BLK:
                    kp[hf, j] = part
                else:
                    kp[hf, j] += part

    def back_block(r0):
        acc = depthwise(gext, 0, 1, rem_, r0)
        for hf in range(2):
            cols = slice(hf * 128, (hf + 1) * 128)
            gin_ref[r0:r0 + BLK, cols] = (dy_ref[r0:r0 + BLK, cols].astype(F32) + acc[hf]).astype(BF16)

    later = range(BLK, ROWS, BLK)
    for r0 in later:
        forward_block(r0)
    for copy in loads[3:]:
        copy.wait()
    feed_forward(0, BLK, ROWS)
    phase_a_wait(0)
    phase_b(0, before)
    for o in range(1, CH):
        feed_forward(o, BLK, ROWS)
    for r0 in later:
        norm_back(r0)
    for r0 in later:
        tap_block(r0)

    halo = phase_b_wait(0, before)
    for hf in range(2):
        ext[hf, :HALO, :] = halo[:, hf * 128:(hf + 1) * 128]
    forward_block(0)
    for o in range(CH):
        feed_forward(o, 0, BLK)
        if o:
            pair_stage(o - 1)
    pair_stage(CH - 1)
    norm_back(0)
    for hf in range(2):
        head[:, hf * 128:(hf + 1) * 128] = gext[hf, :HALO, :].astype(BF16)
    phase_a(1, head)
    tap_block(0)
    for hf in range(2):
        taps = jnp.sum(kp[hf], axis=1)
        gain = jnp.sum(gp[:, hf * 128:(hf + 1) * 128], axis=0, keepdims=True)
        taps = jnp.concatenate([taps, gain, jnp.zeros((64 - K - 1, 128), F32)], axis=0)
        for r in range(8):
            kb[2 * r + hf] = taps[r * 8:r * 8 + 8, :]

    def send_k(i):
        p = lax.rem(q + i, NQ)
        return remote(kb.at[p], rk.at[s], k_s.at[i], k_r.at[s], (z, p * 2))

    def send_z(zp):
        return remote(zs.at[zp], r2.at[z], z_s.at[zp], z_r.at[z], (zp, s))

    def plane_sum(o):
        def got(k):
            remote(r1.at[o, k], r1.at[o, k], p_s.at[o, k], p_r.at[o, k], sibling).wait_recv()

        loop(1, NQ, got)
        acc = tsum[o, rows16(q), :].astype(F32)
        for k in range(1, NQ):
            acc = acc + r1[o, k].astype(F32)
        for j in range(4):
            rh, hf = j // 2, j % 2
            zs[order[o] * 4 + j] = acc[rh * 8:rh * 8 + 8, hf * 128:(hf + 1) * 128]
        for j in range(4):
            zp = order[o] * 4 + j

            @pl.when(zp != z)
            def _(zp=zp):
                send_z(zp).start()

    for o in range(CH):
        plane_sum(o)

    loop(1, NQ, lambda i: send_k(i).start())

    @pl.when(core == 1)
    def _():
        send_k(0).start()

    phase_a_wait(1)
    phase_b(1, after)
    out_ref[...] = (x_ref[...].astype(F32) + oacc_s[...]).astype(BF16)
    back_block(BLK)

    def got_z(i):
        zp = lax.rem(z + i, NZ)
        remote(r2.at[zp], r2.at[zp], z_s.at[zp], z_r.at[zp], sibling).wait_recv()

    loop(1, NZ, got_z)
    total = zs[z]
    for i in range(1, NZ):
        total = total + r2[lax.rem(z + i, NZ)]
    a1[z] = total * FACTOR

    def send_y(i):
        return remote(a1.at[z], a1.at[z], y_s.at[i], y_r.at[z], (lax.rem(z + i, NZ), s))

    for i in FAR_Z:
        send_y(i).start()

    @pl.when(core == 0)
    def _():
        def got(i):
            sp = lax.rem(s + i, NSEQ)
            remote(rk.at[sp], rk.at[sp], k_s.at[0], k_r.at[sp], sibling).wait_recv()

        loop(1, NSEQ, got)
        rk[s] = kb[q]
        acc = rk[0]
        for i in range(1, NSEQ):
            acc = acc + rk[i]
        rz[z] = acc
        loop(1, NZ, lambda i: remote(
            rz.at[z], rz.at[z], kz_s.at[i], kz_r.at[i], (lax.rem(z + i, NZ), s)).start())

    back_block(0)
    back_block(2 * BLK)

    def chunk_of(o):
        return lax.rem(gz + (0, 1, 3, 2)[o], CH)

    def send_q(o, k):
        piece = fin.at[core, chunk_of(o), rows16(q), :]
        return remote(piece, piece, q_s.at[o, k], q_r.at[o, k], (z, chip(k) * 2 + core))

    for o in range(CH):
        h = chunk_of(o)
        for j in range(4):
            zp = h * 4 + j

            @pl.when(zp != z)
            def _(zp=zp):
                remote(a1.at[zp], a1.at[zp], y_s.at[0], y_r.at[zp], sibling).wait_recv()

        top = jnp.concatenate([a1[4 * h], a1[4 * h + 1]], axis=1)
        bottom = jnp.concatenate([a1[4 * h + 2], a1[4 * h + 3]], axis=1)
        fin[core, h, rows16(q), :] = jnp.concatenate([top, bottom], axis=0).astype(BF16)
        loop(0, NQ - 1, lambda i, o=o: send_q(o, offset(i)).start())

    halo_g = phase_b_wait(1, after)
    for hf in range(2):
        gext[hf, ROWS:, :] = halo_g[:, hf * 128:(hf + 1) * 128]
    back_block(3 * BLK)
    stores = [
        pltpu.make_async_copy(src, dst, st_sem.at[i])
        for i, (src, dst) in enumerate((
            (out_ref, out_hbm), (gin_ref, gin_hbm), (gk_ref, gk_hbm), (gg_ref, gg_hbm)))
    ]
    stores[0].start()
    stores[1].start()

    @pl.when(core == 0)
    def _():
        def got(i):
            slot = rz.at[lax.rem(z + NZ - i, NZ)]
            remote(slot, slot, kz_s.at[i], kz_r.at[i], sibling).wait_recv()

        loop(1, NZ, got)
        acc = rz[0]
        for i in range(1, NZ):
            acc = acc + rz[i]
        kf[q] = acc * FACTOR
        loop(1, NSEQ, lambda i: remote(
            kf.at[q], kf.at[q], kf_s.at[i], kf_r.at[q], (z, lax.rem(s + i, NSEQ))).start())

    def send_f(o):
        half = fin.at[core, chunk_of(o)]
        return remote(half, half, f_s.at[o], f_r.at[o], sibling)

    def store(matrix, o):
        part = pl.ds(pl.multiple_of(chunk_of(o) * 256, 256), 256)

        @pl.when(matrix == 0)
        def _():
            pltpu.make_async_copy(fin.at[0, chunk_of(o)], gd_hbm.at[part, :], st_sem.at[4 + o]).start()

        @pl.when(matrix == 1)
        def _():
            pltpu.make_async_copy(fin.at[1, chunk_of(o)], gu_hbm.at[:, part], st_sem.at[8 + o]).start()

    for o in range(CH):
        def got_q(k, o=o):
            qs = lax.rem(xx + 4 - lax.div(k, 4), 4) * 4 + lax.rem(yy + 4 - lax.rem(k, 4), 4)
            piece = fin.at[core, chunk_of(o), rows16(qs), :]
            remote(piece, piece, q_s.at[o, k], q_r.at[o, k], sibling).wait_recv()

        loop(1, NQ, got_q)
        send_f(o).start()
        store(core, o)

    def got_kf(i):
        slot = lax.rem(q + i, NQ)
        remote(kf.at[slot], kf.at[slot], kf_s.at[0], kf_r.at[slot], sibling).wait_recv()

    loop(1, NQ, got_kf)

    @pl.when(core == 1)
    def _():
        got_kf(0)

    for hf in range(2):
        cols = slice(hf * 128, (hf + 1) * 128)
        taps = jnp.concatenate([kf[2 * r + hf] for r in range(8)], axis=0)
        gk_ref[:, cols] = taps[:K, :].astype(BF16)
        gg_ref[:, cols] = taps[K:K + 1, :]
    stores[2].start()
    stores[3].start()
    for o in range(CH):
        half = fin.at[1 - core, chunk_of(o)]
        remote(half, half, f_s.at[o], f_r.at[o], sibling).wait_recv()
        store(1 - core, o)

    for d, src in ((0, tail), (1, head)):
        for i in range(1, 4):
            remote(src, src, a_s.at[d, i], a_r.at[d, i], sibling).wait_send()
        for i in range(1, 8):
            remote(send_b.at[d, i], send_b.at[d, i], b_s.at[d, i], b_r.at[d, i], sibling).wait_send()
    for o in range(CH):
        remote(outbound.at[o], outbound.at[o], c_s.at[o], c_r.at[o], sibling).wait_send()

        def sent(k, o=o):
            slot = tsum.at[o, rows16(chip(k)), :]
            remote(slot, slot, p_s.at[o, k], p_r.at[o, k], sibling).wait_send()
            send_q(o, k).wait_send()

        loop(1, NQ, sent)
        send_f(o).wait_send()
    loop(1, NZ, lambda i: send_z(lax.rem(z + i, NZ)).wait_send())
    loop(1, NZ, lambda i: send_y(i).wait_send())
    loop(1, NQ, lambda i: send_k(i).wait_send())

    @pl.when(core == 1)
    def _():
        send_k(0).wait_send()

    @pl.when(core == 0)
    def _():
        loop(1, NZ, lambda i: remote(
            rz.at[z], rz.at[z], kz_s.at[i], kz_r.at[i], sibling).wait_send())
        loop(1, NSEQ, lambda i: remote(
            kf.at[q], kf.at[q], kf_s.at[i], kf_r.at[q], sibling).wait_send())

    for copy in stores:
        copy.wait()
    for o in range(CH):
        part = pl.ds(pl.multiple_of(chunk_of(o) * 256, 256), 256)
        pltpu.make_async_copy(fin.at[0, chunk_of(o)], gd_hbm.at[part, :], st_sem.at[4 + o]).wait()
        pltpu.make_async_copy(fin.at[1, chunk_of(o)], gu_hbm.at[:, part], st_sem.at[8 + o]).wait()


def finish(*refs):
    ins, outs, held = refs[:5], refs[6:11], refs[12:17]
    gg_i, gg_o, get, put = refs[5], refs[11], refs[17], refs[18]
    loads = [pltpu.make_async_copy(a, b, get.at[i]) for i, (a, b) in enumerate(zip(ins, held))]
    stores = [pltpu.make_async_copy(a, b, put.at[i]) for i, (a, b) in enumerate(zip(held, outs))]
    for copy in loads:
        copy.start()
    gg_o[...] = gg_i[0, :].astype(BF16)
    for load, store in zip(loads, stores):
        load.wait()
        store.start()
    for copy in stores:
        copy.wait()


def per_device(inputs, cotangent, lengths, placed, conv_weight, norm_gain, up_weight, down_weight):
    vm = pl.BlockSpec(memory_space=pltpu.VMEM)
    sm = pl.BlockSpec(memory_space=pltpu.SMEM)
    hb = pl.BlockSpec(memory_space=pltpu.HBM)
    V, D = pltpu.VMEM, pltpu.SemaphoreType.DMA
    out, gin, gk, gg, gu, gd = pl.pallas_call(
        kernel,
        out_shape=(
            jax.ShapeDtypeStruct((ROWS, C), BF16),
            jax.ShapeDtypeStruct((ROWS, C), BF16),
            jax.ShapeDtypeStruct((K, C), BF16),
            jax.ShapeDtypeStruct((1, C), F32),
            jax.ShapeDtypeStruct((C, HID), BF16),
            jax.ShapeDtypeStruct((HID, C), BF16),
        ),
        in_specs=[sm, sm, hb, hb, hb, hb, hb, hb],
        out_specs=(hb,) * 6,
        scratch_shapes=[
            V((ROWS, C), BF16), V((ROWS, C), BF16), V((K, C), BF16), V((1, C), F32),
            V((2, CH, 256, 256), BF16),
            V((ROWS, C), BF16), V((ROWS, C), BF16), V((K, C), F32), V((1, C), F32),
            V((C, HID), BF16), V((HID, C), BF16),
            V((4, HALO, C), BF16), V((4, HALO, C), BF16), V((2, 8, HALO, C), BF16),
            V((8, HALO, C), BF16), V((8, HALO, C), BF16),
            V((HALO, C), BF16),
            V((2, HALO + ROWS, 128), F32), V((2, ROWS + HALO, 128), F32),
            V((ROWS, 128), jnp.int32), V((ROWS, 128), jnp.int32),
            V((ROWS, C), F32), V((ROWS, 128), F32), V((ROWS, C), BF16),
            V((ROWS, C), F32), V((ROWS, C), F32),
            V((CH, 256, 256), F32), V((CH, 256, 256), F32),
            V((CH, 256, 256), BF16), V((CH, 256, 256), BF16), V((CH, 256, 256), BF16),
            V((CH, NQ, 16, 256), BF16),
            V((NZ, 8, 128), F32), V((NZ, 8, 128), F32), V((NZ, 8, 128), F32),
            V((2, K, 8, 128), F32), V((8, C), F32), V((NQ, 8, 128), F32), V((NSEQ, 8, 128), F32),
            V((NZ, 8, 128), F32), V((NQ, 8, 128), F32),
            D((6,)), D((2, 4)), D((2, 4)), D((2, 8)), D((2, 8)), D((CH,)), D((CH,)),
            D((CH, NQ)), D((CH, NQ)), D((NZ,)), D((NZ,)), D((NZ,)), D((NZ,)), D((CH, NQ)), D((CH, NQ)),
            D((CH,)), D((CH,)), D((NQ,)), D((NSEQ,)), D((NZ,)), D((NZ,)), D((NSEQ,)), D((NQ,)), D((12,)),
        ],
        compiler_params=pltpu.CompilerParams(
            collective_id=0, has_side_effects=True, vmem_limit_bytes=VM_BYTES
        ),
    )(
        lengths, placed, inputs.reshape(ROWS, C), cotangent.reshape(ROWS, C), conv_weight,
        norm_gain.reshape(1, C), up_weight, down_weight,
    )
    out, gin, gk, gu, gd, gg = pl.pallas_call(
        finish,
        out_shape=(
            jax.ShapeDtypeStruct((ROWS, C), BF16),
            jax.ShapeDtypeStruct((ROWS, C), BF16),
            jax.ShapeDtypeStruct((K, C), BF16),
            jax.ShapeDtypeStruct((C, HID), BF16),
            jax.ShapeDtypeStruct((HID, C), BF16),
            jax.ShapeDtypeStruct((C,), BF16),
        ),
        in_specs=[hb, hb, hb, hb, hb, vm],
        out_specs=(hb, hb, hb, hb, hb, vm),
        scratch_shapes=[
            V((ROWS, C), BF16), V((ROWS, C), BF16), V((K, C), BF16), V((C, HID), BF16), V((HID, C), BF16),
            D((5,)), D((5,)),
        ],
    )(out, gin, gk, gu, gd, gg)
    return (
        out.reshape(inputs.shape), gin.reshape(inputs.shape), gk, gg, gu, gd,
    )


def solution(mesh):
    tok = P("dp", "seq", None, None)
    return jax.shard_map(
        per_device,
        mesh=mesh,
        in_specs=(tok, tok, P("dp", None), P("dp", None), P(), P(), P(), P()),
        out_specs=(tok, tok, P(), P(), P(), P()),
        check_vma=False,
    )
```

```python
import math

import jax
import jax.numpy as jnp
from jax import lax
from jax.experimental import pallas as pl
from jax.experimental.pallas import tpu as pltpu
from jax.sharding import PartitionSpec as P

MESH = pl.DeviceIdType.MESH
F32 = jnp.float32
BF16 = jnp.bfloat16

EPS = 1e-05
C = 256
HID = 1024
K = 51
ROWS = 256
TRACES = 8
HALO = 64
BLK = 64
NZ, NSEQ, NQ = 16, 32, 16
VM_BYTES = 40 * 2**20
CH = 4
FACTOR = 1.0 / math.sqrt(NZ * NSEQ * ROWS)
GELU_C = math.sqrt(2.0 / math.pi)
GELU_A = 0.044715
FAR_Q = (10, 11, 14, 9, 6, 15, 13, 7, 5, 8, 2, 12, 3, 4, 1)
FAR_Z = (8, 7, 9, 6, 10, 5, 11, 4, 12, 3, 13, 2, 14, 1, 15)


def dot(a, b, ca, cb):
    return lax.dot_general(a, b, (((ca,), (cb,)), ((), ())), preferred_element_type=F32)


def remote(src, dst, send, recv, dev):
    return pltpu.make_async_remote_copy(
        src_ref=src, dst_ref=dst, send_sem=send, recv_sem=recv, device_id=dev, device_id_type=MESH
    )


def loop(lo, hi, body):
    def step(i, carry):
        body(i)
        return carry

    lax.fori_loop(lo, hi, step, 0)


def kernel(
    lengths_hbm, placed_hbm, x_hbm, dy_hbm, w_hbm, gain_hbm, up_hbm, down_hbm,
    out_ref, gin_ref, gk_ref, gg_ref, fin,
    lengths, placed, x_ref, dy_ref, w_ref, gain_ref, up_v, down_v,
    gath0, gath1, send_b, recv0, recv1, head, ext, gext, dep, rem_, normed_s, istd_s, scaled_s,
    gn_s, oacc_s, own, other, outbound, sib, tsum, r1, zs, r2, a1, kp, gp, kb, rk, rz, kf,
    ld_sem, a_s, a_r, b_s, b_r, c_s, c_r, p_s, p_r, z_s, z_r, y_s, y_r, q_s, q_r, f_s, f_r,
    k_s, k_r, kz_s, kz_r, kf_s, kf_r,
):
    z = lax.axis_index("dp")
    s = lax.axis_index("seq")
    core = lax.rem(s, 2)
    q = lax.div(s, 2)
    yy = lax.rem(q, 4)
    xx = lax.div(q, 4)
    g = xx * 2 + core
    gz = lax.div(z, 4)
    sibling = (z, q * 2 + 1 - core)
    gath, recv = (gath0, gath1), (recv0, recv1)

    loads = [
        pltpu.make_async_copy(src, dst, ld_sem.at[i])
        for i, (src, dst) in enumerate((
            (placed_hbm, placed), (lengths_hbm, lengths), (x_hbm, x_ref), (w_hbm, w_ref), (gain_hbm, gain_ref),
            (dy_hbm, dy_ref), (up_hbm, up_v), (down_hbm, down_v)))
    ]
    for copy in loads:
        copy.start()

    bar = pltpu.get_barrier_semaphore()
    for i in FAR_Z:
        pl.semaphore_signal(bar, inc=1, device_id=(lax.rem(z + i, NZ), s), device_id_type=MESH)
    loop(0, NSEQ - 1, lambda i: pl.semaphore_signal(
        bar, inc=1, device_id=(z, lax.rem(s + 1 + lax.rem(i + 19, NSEQ - 1), NSEQ)), device_id_type=MESH))
    loads[0].wait()
    loads[1].wait()

    def target(i):
        gt = lax.rem(g + i, 8)
        return (lax.div(gt, 2) * 4 + yy) * 2 + lax.rem(gt, 2)

    targets = [target(i) for i in range(8)]
    at = [placed[0, t] for t in targets]

    def look(k, found):
        p = placed[0, k]
        return tuple(
            jnp.where(p == at[i % 8] + (-1 if i < 8 else 1), k, f) for i, f in enumerate(found)
        )

    found = lax.fori_loop(0, NSEQ, look, (jnp.int32(0),) * 16)
    before, after = found[:8], found[8:]

    def y_of(slot):
        return lax.rem(lax.div(slot, 2), 4)

    def g_of(slot):
        return lax.div(slot, 8) * 2 + lax.rem(slot, 2)

    pos = at[0] * ROWS + lax.broadcasted_iota(jnp.int32, (ROWS, 128), 0)
    ends, end = [], jnp.int32(0)
    for i in range(TRACES):
        end = end + lengths[0, i]
        ends.append(end)
    start = jnp.zeros((ROWS, 128), jnp.int32)
    for e in ends:
        start = jnp.where(e <= pos, e, start)
    dep[...] = pos - start
    stop = jnp.zeros((ROWS, 128), jnp.int32)
    for e in reversed(ends):
        stop = jnp.where(e > pos, e, stop)
    rem_[...] = stop - 1 - pos
    loads[2].wait()
    for hf in range(2):
        ext[hf, HALO:, :] = x_ref[:, hf * 128:(hf + 1) * 128].astype(F32)
    loads[3].wait()
    loads[4].wait()

    def phase_a(d, src):
        for i in range(1, 4):
            peer = (xx * 4 + lax.rem(yy + i, 4)) * 2 + core
            remote(src, gath[d].at[yy], a_s.at[d, i], a_r.at[d, i], (z, peer)).start()
        gath[d][yy] = src[...]

    def phase_a_wait(d):
        for i in range(1, 4):
            slot = gath[d].at[lax.rem(yy + 4 - i, 4)]
            remote(slot, slot, a_s.at[d, i], a_r.at[d, i], sibling).wait_recv()

    def phase_b(d, source):
        for i in (4, 5, 3, 2, 6, 7, 1):
            send_b[d, i] = gath[d][y_of(source[i])]
            remote(send_b.at[d, i], recv[d].at[g], b_s.at[d, i], b_r.at[d, i], (z, targets[i])).start()
        recv[d][g] = gath[d][y_of(source[0])]

    def phase_b_wait(d, source):
        for i in range(1, 8):
            slot = recv[d].at[lax.rem(g + 8 - i, 8)]
            remote(slot, slot, b_s.at[d, i], b_r.at[d, i], sibling).wait_recv()
        return recv[d][g_of(source[0])].astype(F32)

    pl.semaphore_wait(bar, NSEQ - 1 + NZ - 1)
    tail = x_ref.at[pl.ds(ROWS - HALO, HALO), :]
    phase_a(0, tail)

    def depthwise(src, base, sign, mask_ref, r0):
        m = mask_ref[r0:r0 + BLK, :]
        acc = [jnp.zeros((BLK, 128), F32) for _ in range(2)]
        for j in range(K):
            lo = base + r0 + sign * j
            inside = m >= j
            for hf in range(2):
                win = src[hf, lo:lo + BLK, :] * w_ref[j:j + 1, hf * 128:(hf + 1) * 128]
                acc[hf] = acc[hf] + jnp.where(inside, win, 0.0)
        return acc

    def forward_block(r0):
        a0, a1_ = depthwise(ext, HALO, -1, dep, r0)
        mean = jnp.sum(a0 + a1_, axis=1, keepdims=True) * (1.0 / C)
        a0, a1_ = a0 - mean, a1_ - mean
        var = jnp.sum(a0 * a0 + a1_ * a1_, axis=1, keepdims=True) * (1.0 / C)
        inv = lax.rsqrt(var + EPS)
        istd_s[r0:r0 + BLK, :] = jnp.broadcast_to(inv, (BLK, 128))
        for hf, a in enumerate((a0, a1_)):
            cols = slice(hf * 128, (hf + 1) * 128)
            n = a * inv
            normed_s[r0:r0 + BLK, cols] = n
            scaled_s[r0:r0 + BLK, cols] = (n * gain_ref[0:1, cols]).astype(BF16)

    def rows16(i):
        return pl.ds(pl.multiple_of(i * 16, 16), 16)

    x_to = [lax.rem(xx + i, 4) for i in range(4)]
    y_to = [lax.rem(yy + i, 4) for i in range(4)]

    def chip(k):
        return x_to[k // 4] * 4 + y_to[k % 4]

    def chip_back(k):
        return x_to[-(k // 4) % 4] * 4 + y_to[-(k % 4) % 4]

    order = [lax.rem(gz + i, CH) for i in (2, 1, 3, 0)]

    def feed_forward(o, r0, r1_):
        cols = pl.ds(pl.multiple_of(order[o] * 256, 256), 256)
        up_c = up_v[:, cols]
        down_c = down_v[cols, :]
        sc = scaled_s[r0:r1_, :]
        dy = dy_ref[r0:r1_, :]
        hid = dot(sc, up_c, 1, 0)
        gact = dot(dy, down_c, 1, 1)
        h2 = hid * hid
        th = jnp.tanh(hid * (GELU_C + (GELU_C * GELU_A) * h2))
        h1 = 0.5 + 0.5 * th
        act = hid * h1
        slope = h1 + act * (1.0 - th) * (GELU_C + (3.0 * GELU_C * GELU_A) * h2)
        act = act.astype(BF16)
        gh = (gact * slope).astype(BF16)
        out = dot(act, down_c, 1, 0)
        n = dot(gh, up_c, 1, 1)
        if o == 0:
            oacc_s[r0:r1_, :] = out
            gn_s[r0:r1_, :] = n
        else:
            oacc_s[r0:r1_, :] += out
            gn_s[r0:r1_, :] += n
        gdown = dot(act, dy, 0, 0)
        gup = dot(sc, gh, 0, 0)
        first = core == 0
        mine, theirs = jnp.where(first, gdown, gup), jnp.where(first, gup, gdown)
        if r0:
            own[o] = mine
            other[o] = theirs
        else:
            own[o] += mine
            outbound[o] = (other[o] + theirs).astype(BF16)
            remote(outbound.at[o], sib.at[o], c_s.at[o], c_r.at[o], sibling).start()

    def send_p(u, k):
        qp = chip(k)
        return remote(tsum.at[pl.ds(2 * u, 2), rows16(qp), :], r1.at[u, k], p_s.at[u, k], p_r.at[u],
                      (z, qp * 2 + core))

    def pair_stage(o):
        remote(sib.at[o], sib.at[o], c_s.at[o], c_r.at[o], sibling).wait_recv()
        tsum[o] = (own[o] + sib[o].astype(F32)).astype(BF16)
        if o % 2:
            for k in FAR_Q:
                send_p(o // 2, k).start()

    def norm_back(r0):
        gn = gn_s[r0:r0 + BLK, :]
        nm = normed_s[r0:r0 + BLK, :]
        prod = gn * nm
        part = jnp.sum(prod.reshape(BLK // 8, 8, C), axis=0)
        if r0 == BLK:
            gp[...] = part
        else:
            gp[...] += part
        qv = gn * gain_ref[...]
        qn = prod * gain_ref[...]
        m1 = jnp.sum(qv[:, :128] + qv[:, 128:], axis=1, keepdims=True) * (1.0 / C)
        m2 = jnp.sum(qn[:, :128] + qn[:, 128:], axis=1, keepdims=True) * (1.0 / C)
        t = qv - m1 - nm * m2
        for hf in range(2):
            gext[hf, r0:r0 + BLK, :] = t[:, hf * 128:(hf + 1) * 128] * istd_s[r0:r0 + BLK, :]

    def tap_block(r0):
        m = dep[r0:r0 + BLK, :]
        gc = [gext[hf, r0:r0 + BLK, :] for hf in range(2)]
        for j in range(K):
            lo = HALO + r0 - j
            inside = m >= j
            for hf in range(2):
                v = jnp.where(inside, gc[hf] * ext[hf, lo:lo + BLK, :], 0.0)
                part = jnp.sum(v.reshape(BLK // 8, 8, 128), axis=0)
                if r0 == BLK:
                    kp[hf, j] = part
                else:
                    kp[hf, j] += part

    def back_block(r0):
        acc = depthwise(gext, 0, 1, rem_, r0)
        for hf in range(2):
            cols = slice(hf * 128, (hf + 1) * 128)
            gin_ref[r0:r0 + BLK, cols] = (dy_ref[r0:r0 + BLK, cols].astype(F32) + acc[hf]).astype(BF16)

    later = range(BLK, ROWS, BLK)
    for r0 in later:
        forward_block(r0)
    for copy in loads[5:]:
        copy.wait()
    feed_forward(0, BLK, ROWS)
    phase_a_wait(0)
    phase_b(0, before)
    for o in range(1, CH):
        feed_forward(o, BLK, ROWS)
    for r0 in later:
        norm_back(r0)
    for r0 in later:
        tap_block(r0)

    halo = phase_b_wait(0, before)
    for hf in range(2):
        ext[hf, :HALO, :] = halo[:, hf * 128:(hf + 1) * 128]
    forward_block(0)
    for o in range(CH):
        feed_forward(o, 0, BLK)
        if o:
            pair_stage(o - 1)
    pair_stage(CH - 1)
    norm_back(0)
    for hf in range(2):
        head[:, hf * 128:(hf + 1) * 128] = gext[hf, :HALO, :].astype(BF16)
    phase_a(1, head)
    tap_block(0)
    for hf in range(2):
        taps = jnp.sum(kp[hf], axis=1)
        gain = jnp.sum(gp[:, hf * 128:(hf + 1) * 128], axis=0, keepdims=True)
        taps = jnp.concatenate([taps, gain, jnp.zeros((64 - K - 1, 128), F32)], axis=0)
        for r in range(8):
            kb[2 * r + hf] = taps[r * 8:r * 8 + 8, :]

    def send_k(k):
        p = chip(k) * 2
        slot = lax.rem(p - s + NSEQ, NSEQ)
        return remote(kb.at[chip(k)], rk.at[slot], k_s.at[k], k_r.at[0], (z, p))

    def send_z(zp):
        i = lax.rem(zp - z + NZ, NZ)
        return remote(zs.at[zp], r2.at[i], z_s.at[i], z_r.at[0], (zp, s))

    for u in range(CH // 2):
        got = r1.at[u, pl.ds(1, NQ - 1)]
        remote(got, got, p_s.at[u, 0], p_r.at[u], sibling).wait_recv()
        for v in range(2):
            o = 2 * u + v
            acc = tsum[o, rows16(q), :].astype(F32)
            for k in range(1, NQ):
                acc = acc + r1[u, k, v].astype(F32)
            for j in range(4):
                rh, hf = j // 2, j % 2
                zs[order[o] * 4 + j] = acc[rh * 8:rh * 8 + 8, hf * 128:(hf + 1) * 128]
            for j in range(4):
                zp = order[o] * 4 + j

                @pl.when(zp != z)
                def _(zp=zp):
                    send_z(zp).start()

    for k in range(1, NQ):
        send_k(k).start()

    @pl.when(core == 1)
    def _():
        send_k(0).start()

    phase_a_wait(1)
    phase_b(1, after)
    out_ref[...] = (x_ref[...].astype(F32) + oacc_s[...]).astype(BF16)
    back_block(BLK)

    got = r2.at[pl.ds(1, NZ - 1)]
    remote(got, got, z_s.at[0], z_r.at[0], sibling).wait_recv()
    total = zs[z]
    for i in range(1, NZ):
        total = total + r2[i]
    a1[z] = total * FACTOR

    def send_y(i):
        return remote(a1.at[z], a1.at[z], y_s.at[i], y_r.at[z], (lax.rem(z + i, NZ), s))

    for i in FAR_Z:
        send_y(i).start()

    @pl.when(core == 0)
    def _():
        got = rk.at[pl.ds(1, NSEQ - 1)]
        remote(got, got, k_s.at[0], k_r.at[0], sibling).wait_recv()
        acc = kb[q]
        for i in range(1, NSEQ):
            acc = acc + rk[i]
        rz[z] = acc
        loop(1, NZ, lambda i: remote(
            rz.at[z], rz.at[z], kz_s.at[i], kz_r.at[i], (lax.rem(z + i, NZ), s)).start())

    back_block(0)
    back_block(2 * BLK)

    def chunk_of(o):
        return lax.rem(gz + (0, 1, 3, 2)[o], CH)

    def send_q(o, k):
        piece = fin.at[core, chunk_of(o), rows16(q), :]
        return remote(piece, piece, q_s.at[o, k], q_r.at[o, k], (z, chip(k) * 2 + core))

    for o in range(CH):
        h = chunk_of(o)
        for j in range(4):
            zp = h * 4 + j

            @pl.when(zp != z)
            def _(zp=zp):
                remote(a1.at[zp], a1.at[zp], y_s.at[0], y_r.at[zp], sibling).wait_recv()

        top = jnp.concatenate([a1[4 * h], a1[4 * h + 1]], axis=1)
        bottom = jnp.concatenate([a1[4 * h + 2], a1[4 * h + 3]], axis=1)
        fin[core, h, rows16(q), :] = jnp.concatenate([top, bottom], axis=0).astype(BF16)
        for k in FAR_Q:
            send_q(o, k).start()

    halo_g = phase_b_wait(1, after)
    for hf in range(2):
        gext[hf, ROWS:, :] = halo_g[:, hf * 128:(hf + 1) * 128]
    back_block(3 * BLK)

    @pl.when(core == 0)
    def _():
        def got(i):
            slot = rz.at[lax.rem(z + NZ - i, NZ)]
            remote(slot, slot, kz_s.at[i], kz_r.at[i], sibling).wait_recv()

        loop(1, NZ, got)
        acc = rz[0]
        for i in range(1, NZ):
            acc = acc + rz[i]
        kf[q] = acc * FACTOR
        loop(1, NSEQ, lambda i: remote(
            kf.at[q], kf.at[q], kf_s.at[i], kf_r.at[q], (z, lax.rem(s + i, NSEQ))).start())

    def send_f(o):
        half = fin.at[core, chunk_of(o)]
        return remote(half, half, f_s.at[o], f_r.at[o], sibling)

    for d, src in ((0, tail), (1, head)):
        for i in range(1, 4):
            remote(src, src, a_s.at[d, i], a_r.at[d, i], sibling).wait_send()
        for i in range(1, 8):
            remote(send_b.at[d, i], send_b.at[d, i], b_s.at[d, i], b_r.at[d, i], sibling).wait_send()
    for o in range(CH):
        remote(outbound.at[o], outbound.at[o], c_s.at[o], c_r.at[o], sibling).wait_send()
    for k in range(1, NQ):
        for u in range(CH // 2):
            send_p(u, k).wait_send()
        send_k(k).wait_send()
    for i in range(1, NZ):
        remote(zs.at[0], r2.at[i], z_s.at[i], z_r.at[0], sibling).wait_send()
        send_y(i).wait_send()

    for o in range(CH):
        for k in FAR_Q[::-1]:
            piece = fin.at[core, chunk_of(o), rows16(chip_back(k)), :]
            remote(piece, piece, q_s.at[o, k], q_r.at[o, k], sibling).wait_recv()
        send_f(o).start()

    def got_kf(i):
        slot = lax.rem(q + i, NQ)
        remote(kf.at[slot], kf.at[slot], kf_s.at[0], kf_r.at[slot], sibling).wait_recv()

    loop(1, NQ, got_kf)

    @pl.when(core == 1)
    def _():
        got_kf(0)

    for hf in range(2):
        cols = slice(hf * 128, (hf + 1) * 128)
        taps = jnp.concatenate([kf[2 * r + hf] for r in range(8)], axis=0)
        gk_ref[:, cols] = taps[:K, :].astype(BF16)
        gg_ref[:, cols] = taps[K:K + 1, :]
    for o in range(CH):
        half = fin.at[1 - core, chunk_of(o)]
        remote(half, half, f_s.at[o], f_r.at[o], sibling).wait_recv()

    for o in range(CH):
        for k in range(1, NQ):
            send_q(o, k).wait_send()
        send_f(o).wait_send()

    @pl.when(core == 1)
    def _():
        send_k(0).wait_send()

    @pl.when(core == 0)
    def _():
        loop(1, NZ, lambda i: remote(
            rz.at[z], rz.at[z], kz_s.at[i], kz_r.at[i], sibling).wait_send())
        loop(1, NSEQ, lambda i: remote(
            kf.at[q], kf.at[q], kf_s.at[i], kf_r.at[q], sibling).wait_send())


def finish(out_i, gin_i, gk_i, gg_i, fin, out_o, gin_o, gk_o, gu_o, gd_o, gg_o, sem):
    pairs = [(out_i, out_o), (gin_i, gin_o), (gk_i, gk_o)]
    for h in range(CH):
        part = pl.ds(h * 256, 256)
        pairs += [(fin.at[0, h], gd_o.at[part, :]), (fin.at[1, h], gu_o.at[:, part])]
    copies = [pltpu.make_async_copy(a, b, sem.at[i]) for i, (a, b) in enumerate(pairs)]
    for copy in copies:
        copy.start()
    gg_o[...] = gg_i[0, :].astype(BF16)
    for copy in copies:
        copy.wait()


def per_device(inputs, cotangent, lengths, placed, conv_weight, norm_gain, up_weight, down_weight):
    vm = pl.BlockSpec(memory_space=pltpu.VMEM)
    hb = pl.BlockSpec(memory_space=pltpu.HBM)
    V, D = pltpu.VMEM, pltpu.SemaphoreType.DMA
    held = pl.pallas_call(
        kernel,
        out_shape=(
            V((ROWS, C), BF16), V((ROWS, C), BF16), V((K, C), BF16), V((1, C), F32), V((2, CH, 256, 256), BF16),
        ),
        in_specs=[hb] * 8,
        out_specs=(vm,) * 5,
        scratch_shapes=[
            pltpu.SMEM((1, TRACES), jnp.int32), pltpu.SMEM((1, NSEQ), jnp.int32),
            V((ROWS, C), BF16), V((ROWS, C), BF16), V((K, C), F32), V((1, C), F32),
            V((C, HID), BF16), V((HID, C), BF16),
            V((4, HALO, C), BF16), V((4, HALO, C), BF16), V((2, 8, HALO, C), BF16),
            V((8, HALO, C), BF16), V((8, HALO, C), BF16),
            V((HALO, C), BF16),
            V((2, HALO + ROWS, 128), F32), V((2, ROWS + HALO, 128), F32),
            V((ROWS, 128), jnp.int32), V((ROWS, 128), jnp.int32),
            V((ROWS, C), F32), V((ROWS, 128), F32), V((ROWS, C), BF16),
            V((ROWS, C), F32), V((ROWS, C), F32),
            V((CH, 256, 256), F32), V((CH, 256, 256), F32),
            V((CH, 256, 256), BF16), V((CH, 256, 256), BF16), V((CH, 256, 256), BF16),
            V((CH // 2, NQ, 2, 16, 256), BF16),
            V((NZ, 8, 128), F32), V((NZ, 8, 128), F32), V((NZ, 8, 128), F32),
            V((2, K, 8, 128), F32), V((8, C), F32), V((NQ, 8, 128), F32), V((NSEQ, 8, 128), F32),
            V((NZ, 8, 128), F32), V((NQ, 8, 128), F32),
            D((8,)), D((2, 4)), D((2, 4)), D((2, 8)), D((2, 8)), D((CH,)), D((CH,)),
            D((CH // 2, NQ)), D((CH // 2,)), D((NZ,)), D((1,)), D((NZ,)), D((NZ,)), D((CH, NQ)), D((CH, NQ)),
            D((CH,)), D((CH,)), D((NQ,)), D((1,)), D((NZ,)), D((NZ,)), D((NSEQ,)), D((NQ,)),
        ],
        compiler_params=pltpu.CompilerParams(
            collective_id=0, has_side_effects=True, vmem_limit_bytes=VM_BYTES
        ),
    )(
        *(pltpu.with_memory_space_constraint(a, pltpu.HBM) for a in (
            lengths, placed, inputs.reshape(ROWS, C), cotangent.reshape(ROWS, C), conv_weight,
            norm_gain.reshape(1, C), up_weight, down_weight)),
    )
    out, gin, gk, gu, gd, gg = pl.pallas_call(
        finish,
        out_shape=(
            jax.ShapeDtypeStruct((ROWS, C), BF16),
            jax.ShapeDtypeStruct((ROWS, C), BF16),
            jax.ShapeDtypeStruct((K, C), BF16),
            jax.ShapeDtypeStruct((C, HID), BF16),
            jax.ShapeDtypeStruct((HID, C), BF16),
            jax.ShapeDtypeStruct((C,), BF16),
        ),
        in_specs=[vm] * 5,
        out_specs=(hb, hb, hb, hb, hb, vm),
        scratch_shapes=[D((3 + 2 * CH,))],
        compiler_params=pltpu.CompilerParams(vmem_limit_bytes=2**20),
    )(*held)
    return (
        out.reshape(inputs.shape), gin.reshape(inputs.shape), gk, gg, gu, gd,
    )


def solution(mesh):
    tok = P("dp", "seq", None, None)
    return jax.shard_map(
        per_device,
        mesh=mesh,
        in_specs=(tok, tok, P("dp", None), P("dp", None), P(), P(), P(), P()),
        out_specs=(tok, tok, P(), P(), P(), P()),
        check_vma=False,
    )
```

```python
import math

import jax
import jax.numpy as jnp
from jax import lax
from jax.experimental import pallas as pl
from jax.experimental.pallas import tpu as pltpu
from jax.sharding import PartitionSpec as P

MESH = pl.DeviceIdType.MESH
F32 = jnp.float32
BF16 = jnp.bfloat16

EPS = 1e-05
C = 256
HID = 1024
K = 51
ROWS = 256
TRACES = 8
HALO = 64
BLK = 64
NZ, NSEQ, NQ = 16, 32, 16
VM_BYTES = 40 * 2**20
GROUP = 1
CH = 4
FACTOR = 1.0 / math.sqrt(NZ * NSEQ * ROWS)
GELU_C = math.sqrt(2.0 / math.pi)
GELU_A = 0.044715
FAR_Q = (10, 11, 14, 9, 6, 15, 13, 7, 5, 8, 2, 12, 3, 4, 1)
FAR_Z = (8, 7, 9, 6, 10, 5, 11, 4, 12, 3, 13, 2, 14, 1, 15)


def dot(a, b, ca, cb):
    return lax.dot_general(a, b, (((ca,), (cb,)), ((), ())), preferred_element_type=F32)


def remote(src, dst, send, recv, dev):
    return pltpu.make_async_remote_copy(
        src_ref=src, dst_ref=dst, send_sem=send, recv_sem=recv, device_id=dev, device_id_type=MESH
    )


def loop(lo, hi, body):
    def step(i, carry):
        body(i)
        return carry

    lax.fori_loop(lo, hi, step, 0)


def kernel(
    lengths_hbm, placed_hbm, x_hbm, dy_hbm, w_hbm, gain_hbm, up_hbm, down_hbm,
    out_ref, gin_ref, gk_ref, gg_ref, fin,
    lengths, placed, x_ref, dy_ref, w_ref, gain_ref, up_v, down_v,
    gath00, gath01, gath10, gath11, send_b, recv00, recv01, recv10, recv11, head, ext, gext, dep, rem_, normed_s, istd_s, scaled_s,
    gn_s, oacc_s, own, other, outbound, sib, tsum, r1, zs, r2, a1, kp, gp, kb, rk, rz, kf,
    ld_sem, a_s, a_r, b_s, b_r, c_s, c_r, p_s, p_r, z_s, z_r, y_s, y_r, q_s, q_r, f_s, f_r,
    k_s, k_r, kz_s, kz_r, kf_s, kf_r,
):
    z = lax.axis_index("dp")
    s = lax.axis_index("seq")
    core = lax.rem(s, 2)
    q = lax.div(s, 2)
    yy = lax.rem(q, 4)
    xx = lax.div(q, 4)
    across = (xx * 2 + core, yy * 2 + core)
    along = (yy, xx)
    gz = lax.div(z, 4)
    sibling = (z, q * 2 + 1 - core)
    gath = ((gath00, gath01), (gath10, gath11))
    recv = ((recv00, recv01), (recv10, recv11))

    x_to = [lax.rem(xx + i, 4) for i in range(4)]
    y_to = [lax.rem(yy + i, 4) for i in range(4)]

    def chip(k):
        return x_to[k // 4] * 4 + y_to[k % 4]

    def chip_back(k):
        return x_to[-(k // 4) % 4] * 4 + y_to[-(k % 4) % 4]

    bar = pltpu.get_barrier_semaphore()

    def greet(zp, sp):
        pl.semaphore_signal(bar, inc=1, device_id=(zp, sp), device_id_type=MESH)

    for i in FAR_Z:
        greet(lax.rem(z + i, NZ), s)
    for k in FAR_Q:
        greet(z, chip(k) * 2 + core)
        greet(z, chip(k) * 2 + 1 - core)
    greet(z, sibling[1])
    loads = [
        pltpu.make_async_copy(src, dst, ld_sem.at[i])
        for i, (src, dst) in enumerate((
            (placed_hbm, placed), (lengths_hbm, lengths), (x_hbm, x_ref), (w_hbm, w_ref), (gain_hbm, gain_ref),
            (dy_hbm, dy_ref), (up_hbm, up_v), (down_hbm, down_v)))
    ]
    for copy in loads:
        copy.start()

    pl.semaphore_wait(bar, NSEQ - 1 + NZ - 1)

    def half(hf):
        return pl.ds(hf * 128, 128)

    def send_a(d, hf, i, src):
        sp = ((xx * 4 + y_to[i]) if hf == 0 else (x_to[i] * 4 + yy)) * 2 + core
        return remote(src.at[:, half(hf)], gath[d][hf].at[along[hf]], a_s.at[2 * d + hf, i], a_r.at[2 * d + hf, i],
                      (z, sp))

    def phase_a(d, src):
        for i in (2, 1, 3):
            for hf in range(2):
                send_a(d, hf, i, src).start()

    def phase_a_wait(d):
        for i in range(1, 4):
            for hf in range(2):
                slot = gath[d][hf].at[lax.rem(along[hf] + 4 - i, 4)]
                remote(slot, slot, a_s.at[2 * d + hf, i], a_r.at[2 * d + hf, i], sibling).wait_recv()

    tail = x_hbm.at[pl.ds(ROWS - HALO, HALO), :]
    phase_a(0, tail)
    loads[0].wait()
    loads[1].wait()

    def target(hf, i):
        gt = lax.rem(across[hf] + i, 8)
        chip_of = lax.div(gt, 2) * 4 + yy if hf == 0 else xx * 4 + lax.div(gt, 2)
        return chip_of * 2 + lax.rem(gt, 2)

    targets = [[target(hf, i) for i in range(8)] for hf in range(2)]
    at = [placed[0, t] for t in targets[0] + targets[1][1:]]

    def look(k, found):
        p = placed[0, k]
        return tuple(
            jnp.where(p == at[i % 15] + (-1 if i < 15 else 1), k, f) for i, f in enumerate(found)
        )

    found = lax.fori_loop(0, NSEQ, look, (jnp.int32(0),) * 30)

    def split(f):
        return f[:8], f[:1] + f[8:]

    before, after = split(found[:15]), split(found[15:])

    def x_of(slot):
        return lax.div(slot, 8)

    def y_of(slot):
        return lax.rem(lax.div(slot, 2), 4)

    def along_of(hf, slot):
        return y_of(slot) if hf == 0 else x_of(slot)

    def across_of(hf, slot):
        return (x_of(slot) if hf == 0 else y_of(slot)) * 2 + lax.rem(slot, 2)

    def send_b_(d, hf, i):
        n = 2 * d + hf
        return remote(send_b.at[n, i], recv[d][hf].at[across[hf]], b_s.at[n, i], b_r.at[n, i], (z, targets[hf][i]))

    def phase_b(d, source):
        for i in (4, 5, 3, 2, 6, 7, 1):
            for hf in range(2):
                send_b[2 * d + hf, i] = gath[d][hf][along_of(hf, source[hf][i])]
                send_b_(d, hf, i).start()
        for hf in range(2):
            recv[d][hf][across[hf]] = gath[d][hf][along_of(hf, source[hf][0])]

    def phase_b_wait(d, source):
        for i in range(1, 8):
            for hf in range(2):
                slot = recv[d][hf].at[lax.rem(across[hf] + 8 - i, 8)]
                remote(slot, slot, b_s.at[2 * d + hf, i], b_r.at[2 * d + hf, i], sibling).wait_recv()
        return [recv[d][hf][across_of(hf, source[hf][0])].astype(F32) for hf in range(2)]

    pos = at[0] * ROWS + lax.broadcasted_iota(jnp.int32, (ROWS, 128), 0)
    ends, end = [], jnp.int32(0)
    for i in range(TRACES):
        end = end + lengths[0, i]
        ends.append(end)
    start = jnp.zeros((ROWS, 128), jnp.int32)
    for e in ends:
        start = jnp.where(e <= pos, e, start)
    dep[...] = pos - start
    stop = jnp.zeros((ROWS, 128), jnp.int32)
    for e in reversed(ends):
        stop = jnp.where(e > pos, e, stop)
    rem_[...] = stop - 1 - pos
    loads[2].wait()
    for hf in range(2):
        ext[hf, HALO:, :] = x_ref[:, hf * 128:(hf + 1) * 128].astype(F32)
    for hf in range(2):
        gath[0][hf][along[hf]] = x_ref[ROWS - HALO:, hf * 128:(hf + 1) * 128]
    loads[3].wait()
    loads[4].wait()

    def depthwise(src, base, sign, mask_ref, r0):
        m = mask_ref[r0:r0 + BLK, :]
        acc = [jnp.zeros((BLK, 128), F32) for _ in range(2)]
        for j in range(K):
            lo = base + r0 + sign * j
            inside = m >= j
            for hf in range(2):
                win = src[hf, lo:lo + BLK, :] * w_ref[j:j + 1, hf * 128:(hf + 1) * 128]
                acc[hf] = acc[hf] + jnp.where(inside, win, 0.0)
        return acc

    def forward_block(r0):
        a0, a1_ = depthwise(ext, HALO, -1, dep, r0)
        mean = jnp.sum(a0 + a1_, axis=1, keepdims=True) * (1.0 / C)
        a0, a1_ = a0 - mean, a1_ - mean
        var = jnp.sum(a0 * a0 + a1_ * a1_, axis=1, keepdims=True) * (1.0 / C)
        inv = lax.rsqrt(var + EPS)
        istd_s[r0:r0 + BLK, :] = jnp.broadcast_to(inv, (BLK, 128))
        for hf, a in enumerate((a0, a1_)):
            cols = slice(hf * 128, (hf + 1) * 128)
            n = a * inv
            normed_s[r0:r0 + BLK, cols] = n
            scaled_s[r0:r0 + BLK, cols] = (n * gain_ref[0:1, cols]).astype(BF16)

    def rows16(i):
        return pl.ds(pl.multiple_of(i * 16, 16), 16)

    order = [lax.rem(gz + i, CH) for i in (2, 1, 3, 0)]

    def feed_forward(o, r0, r1_):
        cols = pl.ds(pl.multiple_of(order[o] * 256, 256), 256)
        up_c = up_v[:, cols]
        down_c = down_v[cols, :]
        sc = scaled_s[r0:r1_, :]
        dy = dy_ref[r0:r1_, :]
        hid = dot(sc, up_c, 1, 0)
        gact = dot(dy, down_c, 1, 1)
        h2 = hid * hid
        th = jnp.tanh(hid * (GELU_C + (GELU_C * GELU_A) * h2))
        h1 = 0.5 + 0.5 * th
        act = hid * h1
        slope = h1 + act * (1.0 - th) * (GELU_C + (3.0 * GELU_C * GELU_A) * h2)
        act = act.astype(BF16)
        gh = (gact * slope).astype(BF16)
        out = dot(act, down_c, 1, 0)
        n = dot(gh, up_c, 1, 1)
        if o == 0:
            oacc_s[r0:r1_, :] = out
            gn_s[r0:r1_, :] = n
        else:
            oacc_s[r0:r1_, :] += out
            gn_s[r0:r1_, :] += n
        gdown = dot(act, dy, 0, 0)
        gup = dot(sc, gh, 0, 0)
        first = core == 0
        mine, theirs = jnp.where(first, gdown, gup), jnp.where(first, gup, gdown)
        if r0:
            own[o] = mine
            other[o] = theirs
        else:
            own[o] += mine
            outbound[o] = (other[o] + theirs).astype(BF16)
            remote(outbound.at[o], sib.at[o], c_s.at[o], c_r.at[o], sibling).start()

    def send_p(u, k):
        qp = chip(k)
        return remote(tsum.at[pl.ds(GROUP * u, GROUP), rows16(qp), :], r1.at[u, k], p_s.at[u, k], p_r.at[u],
                      (z, qp * 2 + core))

    def pair_stage(o):
        remote(sib.at[o], sib.at[o], c_s.at[o], c_r.at[o], sibling).wait_recv()
        tsum[o] = (own[o] + sib[o].astype(F32)).astype(BF16)
        if o % GROUP == GROUP - 1:
            for k in FAR_Q:
                send_p(o // GROUP, k).start()

    def norm_back(r0):
        gn = gn_s[r0:r0 + BLK, :]
        nm = normed_s[r0:r0 + BLK, :]
        prod = gn * nm
        part = jnp.sum(prod.reshape(BLK // 8, 8, C), axis=0)
        if r0 == BLK:
            gp[...] = part
        else:
            gp[...] += part
        qv = gn * gain_ref[...]
        qn = prod * gain_ref[...]
        m1 = jnp.sum(qv[:, :128] + qv[:, 128:], axis=1, keepdims=True) * (1.0 / C)
        m2 = jnp.sum(qn[:, :128] + qn[:, 128:], axis=1, keepdims=True) * (1.0 / C)
        t = qv - m1 - nm * m2
        for hf in range(2):
            gext[hf, r0:r0 + BLK, :] = t[:, hf * 128:(hf + 1) * 128] * istd_s[r0:r0 + BLK, :]

    def tap_block(r0):
        m = dep[r0:r0 + BLK, :]
        gc = [gext[hf, r0:r0 + BLK, :] for hf in range(2)]
        for j in range(K):
            lo = HALO + r0 - j
            inside = m >= j
            for hf in range(2):
                v = jnp.where(inside, gc[hf] * ext[hf, lo:lo + BLK, :], 0.0)
                part = jnp.sum(v.reshape(BLK // 8, 8, 128), axis=0)
                if r0 == BLK:
                    kp[hf, j] = part
                else:
                    kp[hf, j] += part

    def back_block(r0):
        acc = depthwise(gext, 0, 1, rem_, r0)
        for hf in range(2):
            cols = slice(hf * 128, (hf + 1) * 128)
            gin_ref[r0:r0 + BLK, cols] = (dy_ref[r0:r0 + BLK, cols].astype(F32) + acc[hf]).astype(BF16)

    later = range(BLK, ROWS, BLK)
    for r0 in later:
        forward_block(r0)
    for copy in loads[5:]:
        copy.wait()
    phase_a_wait(0)
    phase_b(0, before)
    for o in range(CH):
        feed_forward(o, BLK, ROWS)

    halo = phase_b_wait(0, before)
    for hf in range(2):
        ext[hf, :HALO, :] = halo[hf]
    forward_block(0)
    for o in range(CH):
        feed_forward(o, 0, BLK)
        if o:
            pair_stage(o - 1)
    pair_stage(CH - 1)
    for r0 in later:
        norm_back(r0)
    norm_back(0)
    for hf in range(2):
        rows = gext[hf, :HALO, :].astype(BF16)
        head[:, hf * 128:(hf + 1) * 128] = rows
        gath[1][hf][along[hf]] = rows
    phase_a(1, head)
    for r0 in later:
        tap_block(r0)
    tap_block(0)
    for hf in range(2):
        taps = jnp.sum(kp[hf], axis=1)
        gain = jnp.sum(gp[:, hf * 128:(hf + 1) * 128], axis=0, keepdims=True)
        taps = jnp.concatenate([taps, gain, jnp.zeros((64 - K - 1, 128), F32)], axis=0)
        for r in range(8):
            kb[2 * r + hf] = taps[r * 8:r * 8 + 8, :]

    def send_k(k):
        p = chip(k) * 2
        slot = lax.rem(p - s + NSEQ, NSEQ)
        return remote(kb.at[chip(k)], rk.at[slot], k_s.at[k], k_r.at[0], (z, p))

    def send_z(zp):
        i = lax.rem(zp - z + NZ, NZ)
        return remote(zs.at[zp], r2.at[i], z_s.at[i], z_r.at[0], (zp, s))

    for u in range(CH // GROUP):
        got = r1.at[u, pl.ds(1, NQ - 1)]
        remote(got, got, p_s.at[u, 0], p_r.at[u], sibling).wait_recv()
        for v in range(GROUP):
            o = GROUP * u + v
            acc = tsum[o, rows16(q), :].astype(F32)
            for k in range(1, NQ):
                acc = acc + r1[u, k, v].astype(F32)
            for j in range(4):
                rh, hf = j // 2, j % 2
                zs[order[o] * 4 + j] = acc[rh * 8:rh * 8 + 8, hf * 128:(hf + 1) * 128]
            for j in range(4):
                zp = order[o] * 4 + j

                @pl.when(zp != z)
                def _(zp=zp):
                    send_z(zp).start()

    for k in range(1, NQ):
        send_k(k).start()

    @pl.when(core == 1)
    def _():
        send_k(0).start()

    phase_a_wait(1)
    phase_b(1, after)
    out_ref[...] = (x_ref[...].astype(F32) + oacc_s[...]).astype(BF16)
    back_block(BLK)

    got = r2.at[pl.ds(1, NZ - 1)]
    remote(got, got, z_s.at[0], z_r.at[0], sibling).wait_recv()
    total = zs[z]
    for i in range(1, NZ):
        total = total + r2[i]
    a1[z] = total * FACTOR

    def send_y(i):
        return remote(a1.at[z], a1.at[z], y_s.at[i], y_r.at[z], (lax.rem(z + i, NZ), s))

    for i in FAR_Z:
        send_y(i).start()

    @pl.when(core == 0)
    def _():
        got = rk.at[pl.ds(1, NSEQ - 1)]
        remote(got, got, k_s.at[0], k_r.at[0], sibling).wait_recv()
        acc = kb[q]
        for i in range(1, NSEQ):
            acc = acc + rk[i]
        rz[z] = acc
        loop(1, NZ, lambda i: remote(
            rz.at[z], rz.at[z], kz_s.at[i], kz_r.at[i], (lax.rem(z + i, NZ), s)).start())

    back_block(0)
    back_block(2 * BLK)

    def chunk_of(o):
        return lax.rem(gz + (0, 1, 3, 2)[o], CH)

    def send_q(o, k):
        piece = fin.at[core, chunk_of(o), rows16(q), :]
        return remote(piece, piece, q_s.at[o, k], q_r.at[o, k], (z, chip(k) * 2 + core))

    for o in range(CH):
        h = chunk_of(o)
        for j in range(4):
            zp = h * 4 + j

            @pl.when(zp != z)
            def _(zp=zp):
                remote(a1.at[zp], a1.at[zp], y_s.at[0], y_r.at[zp], sibling).wait_recv()

        top = jnp.concatenate([a1[4 * h], a1[4 * h + 1]], axis=1)
        bottom = jnp.concatenate([a1[4 * h + 2], a1[4 * h + 3]], axis=1)
        fin[core, h, rows16(q), :] = jnp.concatenate([top, bottom], axis=0).astype(BF16)
        for k in FAR_Q:
            send_q(o, k).start()

    halo_g = phase_b_wait(1, after)
    for hf in range(2):
        gext[hf, ROWS:, :] = halo_g[hf]
    back_block(3 * BLK)

    @pl.when(core == 0)
    def _():
        def got(i):
            slot = rz.at[lax.rem(z + NZ - i, NZ)]
            remote(slot, slot, kz_s.at[i], kz_r.at[i], sibling).wait_recv()

        loop(1, NZ, got)
        acc = rz[0]
        for i in range(1, NZ):
            acc = acc + rz[i]
        kf[q] = acc * FACTOR
        loop(1, NSEQ, lambda i: remote(
            kf.at[q], kf.at[q], kf_s.at[i], kf_r.at[q], (z, lax.rem(s + i, NSEQ))).start())

    def send_f(o):
        part = fin.at[core, chunk_of(o)]
        return remote(part, part, f_s.at[o], f_r.at[o], sibling)

    for d, src in ((0, tail), (1, head)):
        for hf in range(2):
            for i in range(1, 4):
                send_a(d, hf, i, src).wait_send()
            for i in range(1, 8):
                send_b_(d, hf, i).wait_send()
    for o in range(CH):
        remote(outbound.at[o], outbound.at[o], c_s.at[o], c_r.at[o], sibling).wait_send()
    for k in range(1, NQ):
        for u in range(CH // GROUP):
            send_p(u, k).wait_send()
        send_k(k).wait_send()
    for i in range(1, NZ):
        remote(zs.at[0], r2.at[i], z_s.at[i], z_r.at[0], sibling).wait_send()
        send_y(i).wait_send()

    for o in range(CH):
        for k in FAR_Q[::-1]:
            piece = fin.at[core, chunk_of(o), rows16(chip_back(k)), :]
            remote(piece, piece, q_s.at[o, k], q_r.at[o, k], sibling).wait_recv()
        send_f(o).start()

    def got_kf(i):
        slot = lax.rem(q + i, NQ)
        remote(kf.at[slot], kf.at[slot], kf_s.at[0], kf_r.at[slot], sibling).wait_recv()

    loop(1, NQ, got_kf)

    @pl.when(core == 1)
    def _():
        got_kf(0)

    for hf in range(2):
        cols = slice(hf * 128, (hf + 1) * 128)
        taps = jnp.concatenate([kf[2 * r + hf] for r in range(8)], axis=0)
        gk_ref[:, cols] = taps[:K, :].astype(BF16)
        gg_ref[:, cols] = taps[K:K + 1, :]
    for o in range(CH):
        part = fin.at[1 - core, chunk_of(o)]
        remote(part, part, f_s.at[o], f_r.at[o], sibling).wait_recv()

    for o in range(CH):
        for k in range(1, NQ):
            send_q(o, k).wait_send()
        send_f(o).wait_send()

    @pl.when(core == 1)
    def _():
        send_k(0).wait_send()

    @pl.when(core == 0)
    def _():
        loop(1, NZ, lambda i: remote(
            rz.at[z], rz.at[z], kz_s.at[i], kz_r.at[i], sibling).wait_send())
        loop(1, NSEQ, lambda i: remote(
            kf.at[q], kf.at[q], kf_s.at[i], kf_r.at[q], sibling).wait_send())


def finish(out_i, gin_i, gk_i, gg_i, fin, out_o, gin_o, gk_o, gu_o, gd_o, gg_o, sem):
    pairs = [(out_i, out_o), (gin_i, gin_o), (gk_i, gk_o)]
    for h in range(CH):
        part = pl.ds(h * 256, 256)
        pairs += [(fin.at[0, h], gd_o.at[part, :]), (fin.at[1, h], gu_o.at[:, part])]
    copies = [pltpu.make_async_copy(a, b, sem.at[i]) for i, (a, b) in enumerate(pairs)]
    for copy in copies:
        copy.start()
    gg_o[...] = gg_i[0, :].astype(BF16)
    for copy in copies:
        copy.wait()


def per_device(inputs, cotangent, lengths, placed, conv_weight, norm_gain, up_weight, down_weight):
    vm = pl.BlockSpec(memory_space=pltpu.VMEM)
    hb = pl.BlockSpec(memory_space=pltpu.HBM)
    V, D = pltpu.VMEM, pltpu.SemaphoreType.DMA
    held = pl.pallas_call(
        kernel,
        out_shape=(
            V((ROWS, C), BF16), V((ROWS, C), BF16), V((K, C), BF16), V((1, C), F32), V((2, CH, 256, 256), BF16),
        ),
        in_specs=[hb] * 8,
        out_specs=(vm,) * 5,
        scratch_shapes=[
            pltpu.SMEM((1, TRACES), jnp.int32), pltpu.SMEM((1, NSEQ), jnp.int32),
            V((ROWS, C), BF16), V((ROWS, C), BF16), V((K, C), F32), V((1, C), F32),
            V((C, HID), BF16), V((HID, C), BF16),
            *[V((4, HALO, 128), BF16)] * 4, V((4, 8, HALO, 128), BF16),
            *[V((8, HALO, 128), BF16)] * 4,
            V((HALO, C), BF16),
            V((2, HALO + ROWS, 128), F32), V((2, ROWS + HALO, 128), F32),
            V((ROWS, 128), jnp.int32), V((ROWS, 128), jnp.int32),
            V((ROWS, C), F32), V((ROWS, 128), F32), V((ROWS, C), BF16),
            V((ROWS, C), F32), V((ROWS, C), F32),
            V((CH, 256, 256), F32), V((CH, 256, 256), F32),
            V((CH, 256, 256), BF16), V((CH, 256, 256), BF16), V((CH, 256, 256), BF16),
            V((CH // GROUP, NQ, GROUP, 16, 256), BF16),
            V((NZ, 8, 128), F32), V((NZ, 8, 128), F32), V((NZ, 8, 128), F32),
            V((2, K, 8, 128), F32), V((8, C), F32), V((NQ, 8, 128), F32), V((NSEQ, 8, 128), F32),
            V((NZ, 8, 128), F32), V((NQ, 8, 128), F32),
            D((8,)), D((4, 4)), D((4, 4)), D((4, 8)), D((4, 8)), D((CH,)), D((CH,)),
            D((CH // GROUP, NQ)), D((CH // GROUP,)), D((NZ,)), D((1,)), D((NZ,)), D((NZ,)), D((CH, NQ)), D((CH, NQ)),
            D((CH,)), D((CH,)), D((NQ,)), D((1,)), D((NZ,)), D((NZ,)), D((NSEQ,)), D((NQ,)),
        ],
        compiler_params=pltpu.CompilerParams(
            collective_id=0, has_side_effects=True, vmem_limit_bytes=VM_BYTES
        ),
    )(
        *(pltpu.with_memory_space_constraint(a, pltpu.HBM) for a in (
            lengths, placed, inputs.reshape(ROWS, C), cotangent.reshape(ROWS, C), conv_weight,
            norm_gain.reshape(1, C), up_weight, down_weight)),
    )
    out, gin, gk, gu, gd, gg = pl.pallas_call(
        finish,
        out_shape=(
            jax.ShapeDtypeStruct((ROWS, C), BF16),
            jax.ShapeDtypeStruct((ROWS, C), BF16),
            jax.ShapeDtypeStruct((K, C), BF16),
            jax.ShapeDtypeStruct((C, HID), BF16),
            jax.ShapeDtypeStruct((HID, C), BF16),
            jax.ShapeDtypeStruct((C,), BF16),
        ),
        in_specs=[vm] * 5,
        out_specs=(hb, hb, hb, hb, hb, vm),
        scratch_shapes=[D((3 + 2 * CH,))],
        compiler_params=pltpu.CompilerParams(vmem_limit_bytes=2**20),
    )(*held)
    return (
        out.reshape(inputs.shape), gin.reshape(inputs.shape), gk, gg, gu, gd,
    )


def solution(mesh):
    tok = P("dp", "seq", None, None)
    return jax.shard_map(
        per_device,
        mesh=mesh,
        in_specs=(tok, tok, P("dp", None), P("dp", None), P(), P(), P(), P()),
        out_specs=(tok, tok, P(), P(), P(), P()),
        check_vma=False,
    )
```

```python
import math

import jax
import jax.numpy as jnp
from jax import lax
from jax.experimental import pallas as pl
from jax.experimental.pallas import tpu as pltpu
from jax.sharding import PartitionSpec as P

MESH = pl.DeviceIdType.MESH
F32 = jnp.float32
BF16 = jnp.bfloat16

EPS = 1e-05
C = 256
HID = 1024
K = 51
ROWS = 256
TRACES = 8
HALO = 64
BLK = 64
NZ, NSEQ, NQ = 16, 32, 16
VM_BYTES = 40 * 2**20
GROUP = 1
CH = 4
FACTOR = 1.0 / math.sqrt(NZ * NSEQ * ROWS)
GELU_C = math.sqrt(2.0 / math.pi)
GELU_A = 0.044715
FAR_Q = (10, 11, 14, 9, 6, 15, 13, 7, 5, 8, 2, 12, 3, 4, 1)
FAR_Z = (8, 7, 9, 6, 10, 5, 11, 4, 12, 3, 13, 2, 14, 1, 15)


def dot(a, b, ca, cb):
    return lax.dot_general(a, b, (((ca,), (cb,)), ((), ())), preferred_element_type=F32)


def remote(src, dst, send, recv, dev):
    return pltpu.make_async_remote_copy(
        src_ref=src, dst_ref=dst, send_sem=send, recv_sem=recv, device_id=dev, device_id_type=MESH
    )


def loop(lo, hi, body):
    def step(i, carry):
        body(i)
        return carry

    lax.fori_loop(lo, hi, step, 0)


def kernel(
    lengths_hbm, placed_hbm, x_hbm, dy_hbm, w_hbm, gain_hbm, up_hbm, down_hbm,
    out_ref, gin_ref, gk_ref, gg_ref, fin,
    lengths, placed, x_ref, dy_ref, w_ref, gain_ref, up_v, down_v,
    gath00, gath01, gath10, gath11, send_b, recv00, recv01, recv10, recv11, head, ext, gext, dep, rem_, normed_s, istd_s, scaled_s,
    gn_s, oacc_s, own, other, outbound, sib, tsum, r1, zs, r2, a1, kp, gp, kb, rk, rz, kf,
    ld_sem, a_s, a_r, b_s, b_r, c_s, c_r, p_s, p_r, z_s, z_r, y_s, y_r, q_s, q_r, f_s, f_r,
    k_s, k_r, kz_s, kz_r, kf_s, kf_r,
):
    z = lax.axis_index("dp")
    s = lax.axis_index("seq")
    core = lax.rem(s, 2)
    q = lax.div(s, 2)
    yy = lax.rem(q, 4)
    xx = lax.div(q, 4)
    across = (xx * 2 + core, yy * 2 + core)
    along = (yy, xx)
    gz = lax.div(z, 4)
    sibling = (z, q * 2 + 1 - core)
    gath = ((gath00, gath01), (gath10, gath11))
    recv = ((recv00, recv01), (recv10, recv11))

    x_to = [lax.rem(xx + i, 4) for i in range(4)]
    y_to = [lax.rem(yy + i, 4) for i in range(4)]

    def chip(k):
        return x_to[k // 4] * 4 + y_to[k % 4]

    def chip_back(k):
        return x_to[-(k // 4) % 4] * 4 + y_to[-(k % 4) % 4]

    bar = pltpu.get_barrier_semaphore()

    def greet(zp, sp):
        pl.semaphore_signal(bar, inc=1, device_id=(zp, sp), device_id_type=MESH)

    for i in FAR_Z:
        greet(lax.rem(z + i, NZ), s)
    for k in FAR_Q:
        greet(z, chip(k) * 2 + core)
        greet(z, chip(k) * 2 + 1 - core)
    greet(z, sibling[1])
    loads = [
        pltpu.make_async_copy(src, dst, ld_sem.at[i])
        for i, (src, dst) in enumerate((
            (placed_hbm, placed), (lengths_hbm, lengths), (x_hbm, x_ref), (w_hbm, w_ref), (gain_hbm, gain_ref),
            (dy_hbm, dy_ref), (up_hbm, up_v), (down_hbm, down_v)))
    ]
    for copy in loads:
        copy.start()

    pl.semaphore_wait(bar, NSEQ - 1 + NZ - 1)

    def half(hf):
        return pl.ds(hf * 128, 128)

    def send_a(d, hf, i, src):
        sp = ((xx * 4 + y_to[i]) if hf == 0 else (x_to[i] * 4 + yy)) * 2 + core
        return remote(src.at[:, half(hf)], gath[d][hf].at[along[hf]], a_s.at[2 * d + hf, i], a_r.at[2 * d + hf, i],
                      (z, sp))

    def phase_a(d, src):
        for i in (2, 1, 3):
            for hf in range(2):
                send_a(d, hf, i, src).start()

    def phase_a_wait(d):
        for i in range(1, 4):
            for hf in range(2):
                slot = gath[d][hf].at[lax.rem(along[hf] + 4 - i, 4)]
                remote(slot, slot, a_s.at[2 * d + hf, i], a_r.at[2 * d + hf, i], sibling).wait_recv()

    tail = x_hbm.at[pl.ds(ROWS - HALO, HALO), :]
    phase_a(0, tail)
    loads[0].wait()
    loads[1].wait()

    def target(hf, i):
        gt = lax.rem(across[hf] + i, 8)
        chip_of = lax.div(gt, 2) * 4 + yy if hf == 0 else xx * 4 + lax.div(gt, 2)
        return chip_of * 2 + lax.rem(gt, 2)

    targets = [[target(hf, i) for i in range(8)] for hf in range(2)]
    at = [placed[0, t] for t in targets[0] + targets[1][1:]]

    def look(k, found):
        p = placed[0, k]
        return tuple(
            jnp.where(p == at[i % 15] + (-1 if i < 15 else 1), k, f) for i, f in enumerate(found)
        )

    found = lax.fori_loop(0, NSEQ, look, (jnp.int32(0),) * 30)

    def split(f):
        return f[:8], f[:1] + f[8:]

    before, after = split(found[:15]), split(found[15:])

    def x_of(slot):
        return lax.div(slot, 8)

    def y_of(slot):
        return lax.rem(lax.div(slot, 2), 4)

    def along_of(hf, slot):
        return y_of(slot) if hf == 0 else x_of(slot)

    def across_of(hf, slot):
        return (x_of(slot) if hf == 0 else y_of(slot)) * 2 + lax.rem(slot, 2)

    def send_b_(d, hf, i):
        n = 2 * d + hf
        return remote(send_b.at[n, i], recv[d][hf].at[across[hf]], b_s.at[n, i], b_r.at[n, i], (z, targets[hf][i]))

    def phase_b(d, source):
        for i in (4, 5, 3, 2, 6, 7, 1):
            for hf in range(2):
                send_b[2 * d + hf, i] = gath[d][hf][along_of(hf, source[hf][i])]
                send_b_(d, hf, i).start()
        for hf in range(2):
            recv[d][hf][across[hf]] = gath[d][hf][along_of(hf, source[hf][0])]

    def phase_b_wait(d, source):
        for i in range(1, 8):
            for hf in range(2):
                slot = recv[d][hf].at[lax.rem(across[hf] + 8 - i, 8)]
                remote(slot, slot, b_s.at[2 * d + hf, i], b_r.at[2 * d + hf, i], sibling).wait_recv()
        return [recv[d][hf][across_of(hf, source[hf][0])].astype(F32) for hf in range(2)]

    pos = at[0] * ROWS + lax.broadcasted_iota(jnp.int32, (ROWS, 128), 0)
    ends, end = [], jnp.int32(0)
    for i in range(TRACES):
        end = end + lengths[0, i]
        ends.append(end)
    start = jnp.zeros((ROWS, 128), jnp.int32)
    for e in ends:
        start = jnp.where(e <= pos, e, start)
    dep[...] = pos - start
    stop = jnp.zeros((ROWS, 128), jnp.int32)
    for e in reversed(ends):
        stop = jnp.where(e > pos, e, stop)
    rem_[...] = stop - 1 - pos
    loads[2].wait()
    for hf in range(2):
        ext[hf, HALO:, :] = x_ref[:, hf * 128:(hf + 1) * 128].astype(F32)
    for hf in range(2):
        gath[0][hf][along[hf]] = x_ref[ROWS - HALO:, hf * 128:(hf + 1) * 128]
    loads[3].wait()
    loads[4].wait()

    def depthwise(src, base, sign, mask_ref, r0):
        m = mask_ref[r0:r0 + BLK, :]
        acc = [jnp.zeros((BLK, 128), F32) for _ in range(2)]
        for j in range(K):
            lo = base + r0 + sign * j
            inside = m >= j
            for hf in range(2):
                win = src[hf, lo:lo + BLK, :] * w_ref[j:j + 1, hf * 128:(hf + 1) * 128]
                acc[hf] = acc[hf] + jnp.where(inside, win, 0.0)
        return acc

    def forward_block(r0):
        a0, a1_ = depthwise(ext, HALO, -1, dep, r0)
        mean = jnp.sum(a0 + a1_, axis=1, keepdims=True) * (1.0 / C)
        a0, a1_ = a0 - mean, a1_ - mean
        var = jnp.sum(a0 * a0 + a1_ * a1_, axis=1, keepdims=True) * (1.0 / C)
        inv = lax.rsqrt(var + EPS)
        istd_s[r0:r0 + BLK, :] = jnp.broadcast_to(inv, (BLK, 128))
        for hf, a in enumerate((a0, a1_)):
            cols = slice(hf * 128, (hf + 1) * 128)
            n = a * inv
            normed_s[r0:r0 + BLK, cols] = n
            scaled_s[r0:r0 + BLK, cols] = (n * gain_ref[0:1, cols]).astype(BF16)

    def rows16(i):
        return pl.ds(pl.multiple_of(i * 16, 16), 16)

    order = [lax.rem(gz + i, CH) for i in (2, 1, 3, 0)]

    def feed_forward(o, r0, r1_):
        cols = pl.ds(pl.multiple_of(order[o] * 256, 256), 256)
        up_c = up_v[:, cols]
        down_c = down_v[cols, :]
        sc = scaled_s[r0:r1_, :]
        dy = dy_ref[r0:r1_, :]
        hid = dot(sc, up_c, 1, 0)
        gact = dot(dy, down_c, 1, 1)
        h2 = hid * hid
        th = jnp.tanh(hid * (GELU_C + (GELU_C * GELU_A) * h2))
        h1 = 0.5 + 0.5 * th
        act = hid * h1
        slope = h1 + act * (1.0 - th) * (GELU_C + (3.0 * GELU_C * GELU_A) * h2)
        act = act.astype(BF16)
        gh = (gact * slope).astype(BF16)
        out = dot(act, down_c, 1, 0)
        n = dot(gh, up_c, 1, 1)
        if o == 0:
            oacc_s[r0:r1_, :] = out
            gn_s[r0:r1_, :] = n
        else:
            oacc_s[r0:r1_, :] += out
            gn_s[r0:r1_, :] += n
        gdown = dot(act, dy, 0, 0)
        gup = dot(sc, gh, 0, 0)
        first = core == 0
        mine, theirs = jnp.where(first, gdown, gup), jnp.where(first, gup, gdown)
        if r0:
            own[o] = mine
            other[o] = theirs
        else:
            own[o] += mine
            outbound[o] = (other[o] + theirs).astype(BF16)
            remote(outbound.at[o], sib.at[o], c_s.at[o], c_r.at[o], sibling).start()

    def send_p(u, k):
        qp = chip(k)
        return remote(tsum.at[pl.ds(GROUP * u, GROUP), rows16(qp), :], r1.at[u, k], p_s.at[u, k], p_r.at[u],
                      (z, qp * 2 + core))

    def pair_stage(o):
        remote(sib.at[o], sib.at[o], c_s.at[o], c_r.at[o], sibling).wait_recv()
        tsum[o] = (own[o] + sib[o].astype(F32)).astype(BF16)
        if o % GROUP == GROUP - 1:
            for k in FAR_Q:
                send_p(o // GROUP, k).start()

    def norm_back(r0):
        gn = gn_s[r0:r0 + BLK, :]
        nm = normed_s[r0:r0 + BLK, :]
        prod = gn * nm
        part = jnp.sum(prod.reshape(BLK // 8, 8, C), axis=0)
        if r0 == BLK:
            gp[...] = part
        else:
            gp[...] += part
        qv = gn * gain_ref[...]
        qn = prod * gain_ref[...]
        m1 = jnp.sum(qv[:, :128] + qv[:, 128:], axis=1, keepdims=True) * (1.0 / C)
        m2 = jnp.sum(qn[:, :128] + qn[:, 128:], axis=1, keepdims=True) * (1.0 / C)
        t = qv - m1 - nm * m2
        for hf in range(2):
            gext[hf, r0:r0 + BLK, :] = t[:, hf * 128:(hf + 1) * 128] * istd_s[r0:r0 + BLK, :]

    def tap_block(r0):
        m = dep[r0:r0 + BLK, :]
        gc = [gext[hf, r0:r0 + BLK, :] for hf in range(2)]
        for j in range(K):
            lo = HALO + r0 - j
            inside = m >= j
            for hf in range(2):
                v = jnp.where(inside, gc[hf] * ext[hf, lo:lo + BLK, :], 0.0)
                part = jnp.sum(v.reshape(BLK // 8, 8, 128), axis=0)
                if r0 == BLK:
                    kp[hf, j] = part
                else:
                    kp[hf, j] += part

    def back_block(r0):
        acc = depthwise(gext, 0, 1, rem_, r0)
        for hf in range(2):
            cols = slice(hf * 128, (hf + 1) * 128)
            gin_ref[r0:r0 + BLK, cols] = (dy_ref[r0:r0 + BLK, cols].astype(F32) + acc[hf]).astype(BF16)

    later = range(BLK, ROWS, BLK)
    for r0 in later:
        forward_block(r0)
    for copy in loads[5:]:
        copy.wait()
    phase_a_wait(0)
    phase_b(0, before)
    for o in range(CH):
        feed_forward(o, BLK, ROWS)

    halo = phase_b_wait(0, before)
    for hf in range(2):
        ext[hf, :HALO, :] = halo[hf]
    forward_block(0)
    for o in range(CH):
        feed_forward(o, 0, BLK)
        if o:
            pair_stage(o - 1)
    for r0 in later:
        norm_back(r0)
    norm_back(0)
    pair_stage(CH - 1)
    for hf in range(2):
        rows = gext[hf, :HALO, :].astype(BF16)
        head[:, hf * 128:(hf + 1) * 128] = rows
        gath[1][hf][along[hf]] = rows
    phase_a(1, head)
    for r0 in later:
        tap_block(r0)
    tap_block(0)
    for hf in range(2):
        taps = jnp.sum(kp[hf], axis=1)
        gain = jnp.sum(gp[:, hf * 128:(hf + 1) * 128], axis=0, keepdims=True)
        taps = jnp.concatenate([taps, gain, jnp.zeros((64 - K - 1, 128), F32)], axis=0)
        for r in range(8):
            kb[2 * r + hf] = taps[r * 8:r * 8 + 8, :]

    def send_k(k):
        p = chip(k) * 2
        slot = lax.rem(p - s + NSEQ, NSEQ)
        return remote(kb.at[chip(k)], rk.at[slot], k_s.at[k], k_r.at[0], (z, p))

    def send_z(zp):
        i = lax.rem(zp - z + NZ, NZ)
        return remote(zs.at[zp], r2.at[i], z_s.at[i], z_r.at[0], (zp, s))

    for u in range(CH // GROUP):
        got = r1.at[u, pl.ds(1, NQ - 1)]
        remote(got, got, p_s.at[u, 0], p_r.at[u], sibling).wait_recv()
        for v in range(GROUP):
            o = GROUP * u + v
            acc = tsum[o, rows16(q), :].astype(F32)
            for k in range(1, NQ):
                acc = acc + r1[u, k, v].astype(F32)
            for j in range(4):
                rh, hf = j // 2, j % 2
                zs[order[o] * 4 + j] = acc[rh * 8:rh * 8 + 8, hf * 128:(hf + 1) * 128]
            for j in range(4):
                zp = order[o] * 4 + j

                @pl.when(zp != z)
                def _(zp=zp):
                    send_z(zp).start()

    for k in range(1, NQ):
        send_k(k).start()

    @pl.when(core == 1)
    def _():
        send_k(0).start()

    phase_a_wait(1)
    phase_b(1, after)
    out_ref[...] = (x_ref[...].astype(F32) + oacc_s[...]).astype(BF16)
    back_block(BLK)

    got = r2.at[pl.ds(1, NZ - 1)]
    remote(got, got, z_s.at[0], z_r.at[0], sibling).wait_recv()
    total = zs[z]
    for i in range(1, NZ):
        total = total + r2[i]
    a1[z] = total * FACTOR

    def send_y(i):
        return remote(a1.at[z], a1.at[z], y_s.at[i], y_r.at[z], (lax.rem(z + i, NZ), s))

    for i in FAR_Z:
        send_y(i).start()

    @pl.when(core == 0)
    def _():
        got = rk.at[pl.ds(1, NSEQ - 1)]
        remote(got, got, k_s.at[0], k_r.at[0], sibling).wait_recv()
        acc = kb[q]
        for i in range(1, NSEQ):
            acc = acc + rk[i]
        rz[z] = acc
        loop(1, NZ, lambda i: remote(
            rz.at[z], rz.at[z], kz_s.at[i], kz_r.at[i], (lax.rem(z + i, NZ), s)).start())

    back_block(0)
    back_block(2 * BLK)

    def chunk_of(o):
        return lax.rem(gz + (0, 1, 3, 2)[o], CH)

    def send_q(o, k):
        piece = fin.at[core, chunk_of(o), rows16(q), :]
        return remote(piece, piece, q_s.at[o, k], q_r.at[o, k], (z, chip(k) * 2 + core))

    for o in range(CH):
        h = chunk_of(o)
        for j in range(4):
            zp = h * 4 + j

            @pl.when(zp != z)
            def _(zp=zp):
                remote(a1.at[zp], a1.at[zp], y_s.at[0], y_r.at[zp], sibling).wait_recv()

        top = jnp.concatenate([a1[4 * h], a1[4 * h + 1]], axis=1)
        bottom = jnp.concatenate([a1[4 * h + 2], a1[4 * h + 3]], axis=1)
        fin[core, h, rows16(q), :] = jnp.concatenate([top, bottom], axis=0).astype(BF16)
        for k in FAR_Q:
            send_q(o, k).start()

    halo_g = phase_b_wait(1, after)
    for hf in range(2):
        gext[hf, ROWS:, :] = halo_g[hf]
    back_block(3 * BLK)

    @pl.when(core == 0)
    def _():
        def got(i):
            slot = rz.at[lax.rem(z + NZ - i, NZ)]
            remote(slot, slot, kz_s.at[i], kz_r.at[i], sibling).wait_recv()

        loop(1, NZ, got)
        acc = rz[0]
        for i in range(1, NZ):
            acc = acc + rz[i]
        kf[q] = acc * FACTOR
        loop(1, NSEQ, lambda i: remote(
            kf.at[q], kf.at[q], kf_s.at[i], kf_r.at[q], (z, lax.rem(s + i, NSEQ))).start())

    def send_f(o):
        part = fin.at[core, chunk_of(o)]
        return remote(part, part, f_s.at[o], f_r.at[o], sibling)

    for d, src in ((0, tail), (1, head)):
        for hf in range(2):
            for i in range(1, 4):
                send_a(d, hf, i, src).wait_send()
            for i in range(1, 8):
                send_b_(d, hf, i).wait_send()
    for o in range(CH):
        remote(outbound.at[o], outbound.at[o], c_s.at[o], c_r.at[o], sibling).wait_send()
    for k in range(1, NQ):
        for u in range(CH // GROUP):
            send_p(u, k).wait_send()
        send_k(k).wait_send()
    for i in range(1, NZ):
        remote(zs.at[0], r2.at[i], z_s.at[i], z_r.at[0], sibling).wait_send()
        send_y(i).wait_send()

    for o in range(CH):
        for k in FAR_Q[::-1]:
            piece = fin.at[core, chunk_of(o), rows16(chip_back(k)), :]
            remote(piece, piece, q_s.at[o, k], q_r.at[o, k], sibling).wait_recv()
        send_f(o).start()

    def got_kf(i):
        slot = lax.rem(q + i, NQ)
        remote(kf.at[slot], kf.at[slot], kf_s.at[0], kf_r.at[slot], sibling).wait_recv()

    loop(1, NQ, got_kf)

    @pl.when(core == 1)
    def _():
        got_kf(0)

    for hf in range(2):
        cols = slice(hf * 128, (hf + 1) * 128)
        taps = jnp.concatenate([kf[2 * r + hf] for r in range(8)], axis=0)
        gk_ref[:, cols] = taps[:K, :].astype(BF16)
        gg_ref[:, cols] = taps[K:K + 1, :]

    for o in range(CH):
        for k in range(1, NQ):
            send_q(o, k).wait_send()
        send_f(o).wait_send()

    @pl.when(core == 1)
    def _():
        send_k(0).wait_send()

    @pl.when(core == 0)
    def _():
        loop(1, NZ, lambda i: remote(
            rz.at[z], rz.at[z], kz_s.at[i], kz_r.at[i], sibling).wait_send())
        loop(1, NSEQ, lambda i: remote(
            kf.at[q], kf.at[q], kf_s.at[i], kf_r.at[q], sibling).wait_send())

    for o in range(CH):
        part = fin.at[1 - core, chunk_of(o)]
        remote(part, part, f_s.at[o], f_r.at[o], sibling).wait_recv()


def finish(out_i, gin_i, gk_i, gg_i, fin, out_o, gin_o, gk_o, gu_o, gd_o, gg_o, sem):
    pairs = [(out_i, out_o), (gin_i, gin_o), (gk_i, gk_o)]
    for h in range(CH):
        part = pl.ds(h * 256, 256)
        pairs += [(fin.at[0, h], gd_o.at[part, :]), (fin.at[1, h], gu_o.at[:, part])]
    copies = [pltpu.make_async_copy(a, b, sem.at[i]) for i, (a, b) in enumerate(pairs)]
    for copy in copies:
        copy.start()
    gg_o[...] = gg_i[0, :].astype(BF16)
    for copy in copies:
        copy.wait()


def per_device(inputs, cotangent, lengths, placed, conv_weight, norm_gain, up_weight, down_weight):
    vm = pl.BlockSpec(memory_space=pltpu.VMEM)
    hb = pl.BlockSpec(memory_space=pltpu.HBM)
    V, D = pltpu.VMEM, pltpu.SemaphoreType.DMA
    held = pl.pallas_call(
        kernel,
        out_shape=(
            V((ROWS, C), BF16), V((ROWS, C), BF16), V((K, C), BF16), V((1, C), F32), V((2, CH, 256, 256), BF16),
        ),
        in_specs=[hb] * 8,
        out_specs=(vm,) * 5,
        scratch_shapes=[
            pltpu.SMEM((1, TRACES), jnp.int32), pltpu.SMEM((1, NSEQ), jnp.int32),
            V((ROWS, C), BF16), V((ROWS, C), BF16), V((K, C), F32), V((1, C), F32),
            V((C, HID), BF16), V((HID, C), BF16),
            *[V((4, HALO, 128), BF16)] * 4, V((4, 8, HALO, 128), BF16),
            *[V((8, HALO, 128), BF16)] * 4,
            V((HALO, C), BF16),
            V((2, HALO + ROWS, 128), F32), V((2, ROWS + HALO, 128), F32),
            V((ROWS, 128), jnp.int32), V((ROWS, 128), jnp.int32),
            V((ROWS, C), F32), V((ROWS, 128), F32), V((ROWS, C), BF16),
            V((ROWS, C), F32), V((ROWS, C), F32),
            V((CH, 256, 256), F32), V((CH, 256, 256), F32),
            V((CH, 256, 256), BF16), V((CH, 256, 256), BF16), V((CH, 256, 256), BF16),
            V((CH // GROUP, NQ, GROUP, 16, 256), BF16),
            V((NZ, 8, 128), F32), V((NZ, 8, 128), F32), V((NZ, 8, 128), F32),
            V((2, K, 8, 128), F32), V((8, C), F32), V((NQ, 8, 128), F32), V((NSEQ, 8, 128), F32),
            V((NZ, 8, 128), F32), V((NQ, 8, 128), F32),
            D((8,)), D((4, 4)), D((4, 4)), D((4, 8)), D((4, 8)), D((CH,)), D((CH,)),
            D((CH // GROUP, NQ)), D((CH // GROUP,)), D((NZ,)), D((1,)), D((NZ,)), D((NZ,)), D((CH, NQ)), D((CH, NQ)),
            D((CH,)), D((CH,)), D((NQ,)), D((1,)), D((NZ,)), D((NZ,)), D((NSEQ,)), D((NQ,)),
        ],
        compiler_params=pltpu.CompilerParams(
            collective_id=0, has_side_effects=True, vmem_limit_bytes=VM_BYTES
        ),
    )(
        *(pltpu.with_memory_space_constraint(a, pltpu.HBM) for a in (
            lengths, placed, inputs.reshape(ROWS, C), cotangent.reshape(ROWS, C), conv_weight,
            norm_gain.reshape(1, C), up_weight, down_weight)),
    )
    out, gin, gk, gu, gd, gg = pl.pallas_call(
        finish,
        out_shape=(
            jax.ShapeDtypeStruct((ROWS, C), BF16),
            jax.ShapeDtypeStruct((ROWS, C), BF16),
            jax.ShapeDtypeStruct((K, C), BF16),
            jax.ShapeDtypeStruct((C, HID), BF16),
            jax.ShapeDtypeStruct((HID, C), BF16),
            jax.ShapeDtypeStruct((C,), BF16),
        ),
        in_specs=[vm] * 5,
        out_specs=(hb, hb, hb, hb, hb, vm),
        scratch_shapes=[D((3 + 2 * CH,))],
        compiler_params=pltpu.CompilerParams(vmem_limit_bytes=2**20),
    )(*held)
    return (
        out.reshape(inputs.shape), gin.reshape(inputs.shape), gk, gg, gu, gd,
    )


def solution(mesh):
    tok = P("dp", "seq", None, None)
    return jax.shard_map(
        per_device,
        mesh=mesh,
        in_specs=(tok, tok, P("dp", None), P("dp", None), P(), P(), P(), P()),
        out_specs=(tok, tok, P(), P(), P(), P()),
        check_vma=False,
    )
```
